512 devices in a mesh: dp: 32 (over x_hi, z, core), fsdp: 16 (over x_lo, y).
Axes of the slice: x: 4 (x_hi: 2, x_lo: 2; x = x_hi * 2 + x_lo), y: 8, z: 8, core: 2. Of those that a mesh axis runs over, the one named last changes fastest.
Arguments:
- states: bfloat16 [512, 2, 128, 64], P(('dp', 'fsdp')), may hold values from -6 to 6
- adjoint: float32 [512, 128, 64], P(('dp', 'fsdp')), may hold values from -6 to 6
- grid_step_index: int32 [512], P(('dp', 'fsdp')), may hold values from 3 to 26
- input_weight: bfloat16 [64, 1536], replicated, may hold values from -0.75 to 0.75
- timestep_weight: bfloat16 [256, 4608], P('fsdp'), may hold values from -0.375 to 0.375
- query_key_value_weight: bfloat16 [1536, 2304], P('fsdp'), may hold values from -0.15625 to 0.15625
- projection_weight: bfloat16 [768, 1536], P('fsdp'), may hold values from -0.21875 to 0.21875
- down_factor: bfloat16 [768, 64], P('fsdp'), may hold values from -0.21875 to 0.21875
- up_factor: bfloat16 [64, 1536], P('fsdp'), may hold values from -0.75 to 0.75
- query_norm_gain: float32 [64], replicated, may hold values from 0.5 to 1.5
- key_norm_gain: float32 [64], replicated, may hold values from 0.5 to 1.5
- final_norm_gain: float32 [1536], replicated, may hold values from 0.1 to 1.9
- output_weight: bfloat16 [1536, 64], replicated, may hold values from -0.15625 to 0.15625
Outputs:
- adjoint_out: float32 [512, 128, 64], P(('dp', 'fsdp'))
- down_factor_gradient: float32 [768, 64], P('fsdp')
- up_factor_gradient: float32 [64, 1536], P('fsdp')
The draws below stay inside these ranges and needn't reach their ends.
Inputs may be any that keep to these rules, and one draw needn't show every extreme that they name: `grid_step_index`: each sample's adjoint stands at grid time (k + 1) / 28.
All inputs are finite; a program needn't handle non-finite values.
Results may differ from the reference program's by a relative error of at most 0.019.
Values may be sent and summed in bfloat16 or wider, within the bound.
No kernel may reach another device: no remote copies, remote signals or barrier semaphores. Data moves between devices by JAX's collectives and lax.ppermute only.
A program may use at most 64 MiB of HBM per device.

```python
import math
from functools import partial
import jax
import jax.numpy as jnp
from jax import lax

MODEL_WIDTH = 1536
HEADS = 12
HEAD_DIM = 64
CHAN = 64
TIME_FEAT = 256
UPDATE_RANK = 64
STEPS = 28
LEN = 128
ATTENTION_WIDTH = 768
SAMPLES = 512


def set_ends(values, own_key, smallest, largest):
    place = [jax.random.randint(jax.random.fold_in(own_key, axis), (), 0, length) for axis, length in enumerate(values.shape)]
    widest = values.shape.index(max(values.shape))
    neighbour = place[:widest] + [(place[widest] + 1) % values.shape[widest]] + place[widest + 1:]
    return values.at[tuple(place)].set(smallest).at[tuple(neighbour)].set(largest)


def shard_levels(own_key, extent, shards, smallest, high):
    factor_of = 1.0
    for dim, blocks in shards:
        draws = jax.random.uniform(jax.random.fold_in(jax.random.fold_in(own_key, 6), dim), (blocks,), jnp.float32, smallest / len(shards), high / len(shards))
        factor_of = factor_of * jnp.repeat(jnp.exp(draws), extent[dim] // blocks).reshape((-1,) + (1,) * (len(extent) - 1 - dim))
    return factor_of


def centred(own_key, shape, deviation, most, pieces=(), kind=jnp.bfloat16):
    values = jax.random.normal(own_key, shape, jnp.float32) * deviation
    if len(pieces) > 0:
        values = shard_levels(own_key, shape, pieces, -0.22, 0.18) * values
    return jnp.clip(values, min=-most, max=most).astype(kind)


def setup_inputs(seed: int = 0) -> dict:
    seeds = jax.random.split(jax.random.key(seed), 14)
    states = centred(seeds[0], (SAMPLES, 2, LEN, CHAN), 1.0, 6.0, ((0, 512),))
    adjoint = centred(seeds[1], (SAMPLES, LEN, CHAN), 1.0, 6.0, ((0, 512),), jnp.float32)
    grid_step_index = set_ends(jax.random.randint(seeds[2], (SAMPLES,), 3, 27), jax.random.fold_in(seeds[2], 1), 3, 26).astype(jnp.int32)
    input_weight = centred(seeds[3], (CHAN, MODEL_WIDTH), CHAN ** -0.5, 0.75)
    timestep_weight = centred(seeds[4], (TIME_FEAT, 3 * MODEL_WIDTH), TIME_FEAT ** -0.5, 0.375, ((0, 16),))
    query_key_value_weight = centred(seeds[5], (MODEL_WIDTH, 3 * ATTENTION_WIDTH), MODEL_WIDTH ** -0.5, 0.15625, ((0, 16),))
    projection_weight = centred(seeds[6], (ATTENTION_WIDTH, MODEL_WIDTH), ATTENTION_WIDTH ** -0.5, 0.21875, ((0, 16),))
    down_factor = centred(seeds[7], (ATTENTION_WIDTH, UPDATE_RANK), ATTENTION_WIDTH ** -0.5, 0.21875, ((0, 16),))
    up_factor = centred(seeds[8], (UPDATE_RANK, MODEL_WIDTH), UPDATE_RANK ** -0.5, 0.75, ((0, 16),))
    query_norm_gain = jnp.clip(1.0 + 0.1 * jax.random.normal(seeds[9], (HEAD_DIM,), jnp.float32), 0.5, 1.5)
    key_norm_gain = jnp.clip(1.0 + 0.1 * jax.random.normal(seeds[10], (HEAD_DIM,), jnp.float32), 0.5, 1.5)
    final_norm_gain = jnp.clip(1.0 + 0.18 * jax.random.normal(seeds[11], (MODEL_WIDTH,), jnp.float32), 0.1, 1.9)
    output_weight = centred(seeds[12], (MODEL_WIDTH, CHAN), MODEL_WIDTH ** -0.5, 0.15625)
    return {"states": states, "adjoint": adjoint, "grid_step_index": grid_step_index, "input_weight": input_weight, "timestep_weight": timestep_weight, "query_key_value_weight": query_key_value_weight, "projection_weight": projection_weight, "down_factor": down_factor, "up_factor": up_factor, "query_norm_gain": query_norm_gain, "key_norm_gain": key_norm_gain, "final_norm_gain": final_norm_gain, "output_weight": output_weight}


def normalize(values):
    return values * lax.rsqrt(lax.optimization_barrier(jnp.mean(values * values, axis=-1, keepdims=True)) + 1e-06)

def time_features(upper_time):
    halves = TIME_FEAT // 2
    frequency = jnp.exp(-math.log(10000.0) * jnp.arange(halves, dtype=jnp.float32) / halves)
    angles = 1000.0 * upper_time * frequency
    return jnp.concatenate([jnp.cos(angles), jnp.sin(angles)]).astype(jnp.bfloat16)

def modulation(upper_time, timestep_weight, width):
    mod_all = jnp.dot(time_features(upper_time)[None, :], timestep_weight, preferred_element_type=jnp.float32)[0]
    return (mod_all[:width], mod_all[width:2 * width], mod_all[2 * width:])

def prelude(latent, input_weight, shift_vec, scale_vec):
    hidden_state = jnp.dot(latent.astype(jnp.bfloat16), input_weight, preferred_element_type=jnp.float32)
    normed = (normalize(hidden_state) * (1.0 + scale_vec) + shift_vec).astype(jnp.bfloat16)
    return (hidden_state, normed)

def mixing(query_key_value_rows, query_norm_gain, key_norm_gain, inner_width):
    tokens_here = query_key_value_rows.shape[0]
    shaped = (tokens_here, HEADS, HEAD_DIM)
    queries = (normalize(query_key_value_rows[:, :inner_width].reshape(shaped)) * query_norm_gain).astype(jnp.bfloat16)
    keyset = (normalize(query_key_value_rows[:, inner_width:2 * inner_width].reshape(shaped)) * key_norm_gain).astype(jnp.bfloat16)
    valueset = query_key_value_rows[:, 2 * inner_width:].reshape(shaped).astype(jnp.bfloat16)
    scores = jnp.einsum('qhd,khd->hqk', queries.astype(jnp.float32), keyset.astype(jnp.float32)) / math.sqrt(HEAD_DIM)
    expscore = jnp.exp(scores)
    attention = (expscore / lax.optimization_barrier(jnp.sum(expscore, axis=-1, keepdims=True))).astype(jnp.bfloat16)
    blended_mix = jnp.einsum('hqk,khd->qhd', attention.astype(jnp.float32), valueset.astype(jnp.float32))
    return blended_mix.reshape(tokens_here, inner_width).astype(jnp.bfloat16)

def finish(projected, hidden_state, gate_vector, final_norm_gain, output_weight):
    normed = (normalize(hidden_state + gate_vector * projected) * final_norm_gain).astype(jnp.bfloat16)
    return jnp.dot(normed, output_weight, preferred_element_type=jnp.float32)

def advance_step(query_key_value_rows, hidden_state, backward_preamble, current_adjoint, upper_time, gate_vector, query_key_value_weight, projection_weight, down_factor, up_factor, query_norm_gain, key_norm_gain, final_norm_gain, output_weight, sample_batch):
    inner_width = projection_weight.shape[0]
    blended_mix, back_mix = jax.vjp(partial(mixing, query_norm_gain=query_norm_gain, key_norm_gain=key_norm_gain, inner_width=inner_width), query_key_value_rows)
    base_projection = jnp.dot(blended_mix, projection_weight, preferred_element_type=jnp.float32)
    lowrank_update = jnp.dot(blended_mix, down_factor, preferred_element_type=jnp.float32).astype(jnp.bfloat16)
    adjusted_projection = base_projection + jnp.dot(lowrank_update, up_factor, preferred_element_type=jnp.float32)
    tail = partial(finish, gate_vector=gate_vector, final_norm_gain=final_norm_gain, output_weight=output_weight)
    base_vel, back_base = jax.vjp(tail, base_projection, hidden_state)
    adjusted_vel, back_adjusted = jax.vjp(lambda projected: tail(projected, hidden_state), adjusted_projection)
    sigma = jnp.sqrt(2.0 * (1.0 - upper_time) / upper_time)
    residual = 2.0 / sigma * (adjusted_vel - base_vel) + sigma * current_adjoint
    adjusted_gradient = back_adjusted(4.0 * residual / (sigma * sample_batch))[0].astype(jnp.bfloat16)
    up_factor_gradient = jnp.dot(lowrank_update.T, adjusted_gradient, preferred_element_type=jnp.float32)
    lowrank_gradient = jnp.dot(adjusted_gradient, up_factor.T, preferred_element_type=jnp.float32).astype(jnp.bfloat16)
    down_factor_gradient = jnp.dot(blended_mix.T, lowrank_gradient, preferred_element_type=jnp.float32)
    proj_grad, hidden_grad = back_base(current_adjoint)
    blend_grad = jnp.dot(proj_grad.astype(jnp.bfloat16), projection_weight.T, preferred_element_type=jnp.float32).astype(jnp.bfloat16)
    qkv_grad = back_mix(blend_grad)[0]
    normed_grad = jnp.dot(qkv_grad.astype(jnp.bfloat16), query_key_value_weight.T, preferred_element_type=jnp.float32).astype(jnp.bfloat16)
    latent_grad = backward_preamble((hidden_grad, normed_grad))[0]
    adjoint_next = current_adjoint + (2.0 * latent_grad - current_adjoint / upper_time) / STEPS
    return (adjoint_next, down_factor_gradient, up_factor_gradient)

def reference(states, adjoint, grid_step_index, input_weight, timestep_weight, query_key_value_weight, projection_weight, down_factor, up_factor, query_norm_gain, key_norm_gain, final_norm_gain, output_weight):
    sample_batch = states.shape[0]
    width = input_weight.shape[1]

    def per_sample(running, inputs):
        down_total, up_total = running
        state_pair, current_adjoint, sample_step = inputs
        for turn_index in range(2):
            upper_time = (sample_step + 1 - turn_index).astype(jnp.float32) / STEPS
            shift_vec, scale_vec, gate_vector = modulation(upper_time, timestep_weight, width)
            forward_output, backward_preamble = jax.vjp(partial(prelude, input_weight=input_weight, shift_vec=shift_vec, scale_vec=scale_vec), state_pair[turn_index].astype(jnp.float32))
            query_key_value_rows = jnp.dot(forward_output[1], query_key_value_weight, preferred_element_type=jnp.float32)
            current_adjoint, down_factor_gradient, up_factor_gradient = advance_step(query_key_value_rows, forward_output[0], backward_preamble, current_adjoint, upper_time, gate_vector, query_key_value_weight, projection_weight, down_factor, up_factor, query_norm_gain, key_norm_gain, final_norm_gain, output_weight, sample_batch)
            down_total = down_total + down_factor_gradient
            up_total = up_total + up_factor_gradient
        return ((down_total, up_total), current_adjoint)
    initial_state = (jnp.zeros(down_factor.shape, jnp.float32), jnp.zeros(up_factor.shape, jnp.float32))
    totals, adjoint_out = lax.scan(per_sample, initial_state, (states, adjoint, grid_step_index))
    return (adjoint_out, totals[0], totals[1])
```

```python
import math

import jax
import jax.numpy as jnp
from jax import lax
from jax.experimental import pallas as pl
from jax.experimental.pallas import tpu as pltpu
from jax.sharding import PartitionSpec as P

HEAD_DIM = 64
TIME_FEAT = 256
STEPS = 28
LANES = 128
EPS = 1e-06
BF = jnp.bfloat16
F32 = jnp.float32


def dot_nn(a, b):
    return lax.dot_general(a, b, (((1,), (0,)), ((), ())), preferred_element_type=F32)


def dot_nt(a, b):
    return lax.dot_general(a, b, (((1,), (1,)), ((), ())), preferred_element_type=F32)


def dot_tn(a, b):
    return lax.dot_general(a, b, (((0,), (0,)), ((), ())), preferred_element_type=F32)


def step_pair_kernel(
    core_ref,
    coef_ref,
    own_ref,
    other_ref,
    normed_ref,
    hidden_ref,
    adjoint_ref,
    scale1_ref,
    gate_ref,
    down_ref,
    up_ref,
    qgain_ref,
    kgain_ref,
    fgain_ref,
    wout_ref,
    win_ref,
    adjoint_out_ref,
    down_out_ref,
    up_out_ref,
    weights,
    sems,
    qn,
    qz,
    qr,
    kn,
    kz,
    kr,
    vn,
    att,
    blended,
    base_u,
    adj_u,
    base_vel,
    adj_vel,
    lowrank,
    adj_grad,
    low_grad,
):
    tokens = adjoint_ref.shape[0]
    rows = 2 * tokens
    width = hidden_ref.shape[1]
    half = weights.shape[3]
    shards = weights.shape[1]
    per_qkv = width // shards
    inner = 2 * half
    per_proj = inner // shards
    pairs = half // LANES
    core = core_ref[0]

    copy_own = pltpu.make_async_copy(own_ref, weights.at[core], sems.at[0])
    copy_other = pltpu.make_async_copy(other_ref, weights.at[1 - core], sems.at[1])
    copy_own.start()
    copy_other.start()

    lane = lax.broadcasted_iota(jnp.int32, (1, LANES), 1)
    even_f = (lane < HEAD_DIM).astype(F32)
    even = even_f.astype(BF)
    odd = (1.0 - even_f).astype(BF)
    row_i = lax.broadcasted_iota(jnp.int32, (2 * LANES, LANES), 0) & (LANES - 1)
    col_i = lax.broadcasted_iota(jnp.int32, (2 * LANES, LANES), 1)
    same = ((row_i >= HEAD_DIM) == (col_i >= HEAD_DIM)).astype(F32)
    averager = (same * (1.0 / HEAD_DIM)).astype(BF)

    def head_mean(values):
        high = values.astype(BF)
        low = (values - high.astype(F32)).astype(BF)
        return dot_nn(jnp.concatenate([high, low], axis=1), averager)

    def split_heads(tile):
        return jnp.concatenate([tile * even, tile * odd], axis=0)

    def qkv_block(h, part):
        return weights[h, :, part * per_qkv : (part + 1) * per_qkv, :].reshape(width, half)

    def proj_block(h, b):
        start = 3 * per_qkv + b * per_proj
        return weights[h, :, start : start + per_proj, :].reshape(inner, half)

    copy_own.wait()
    copy_other.wait()

    normed = normed_ref[...]
    for h in range(2):
        for part, gain_ref, n_ref, z_ref, r_ref in (
            (0, qgain_ref, qn, qz, qr),
            (1, kgain_ref, kn, kz, kr),
        ):
            raw = dot_nn(normed, qkv_block(h, part))
            for p in range(pairs):
                x = raw[:, p * LANES : (p + 1) * LANES]
                r = lax.rsqrt(head_mean(x * x) + EPS)
                z = x * r
                z_ref[h * pairs + p] = z
                r_ref[h * pairs + p] = r
                n_ref[h * pairs + p] = (z * gain_ref[...]).astype(BF)
        raw = dot_nn(normed, qkv_block(h, 2)).astype(BF)
        for p in range(pairs):
            vn[h * pairs + p] = raw[:, p * LANES : (p + 1) * LANES]

    for i in range(2 * pairs):
        for j in range(2):
            rs = slice(j * tokens, (j + 1) * tokens)
            score = dot_nt(split_heads(qn[i, rs, :]), kn[i, rs, :]) * (1.0 / math.sqrt(HEAD_DIM))
            e = jnp.exp(score)
            a = e * (1.0 / jnp.sum(e, axis=-1, keepdims=True))
            att[i, j] = a
            ab = a.astype(BF)
            mixed = dot_nn(
                jnp.concatenate([ab[:tokens], ab[tokens:]], axis=1), split_heads(vn[i, rs, :])
            )
            blended[rs, i * LANES : (i + 1) * LANES] = mixed.astype(BF)

    low = dot_nn(blended[...], down_ref[...]).astype(BF)
    lowrank[...] = low
    for h in range(2):
        for b in range(2):
            cols = slice((2 * h + b) * half, (2 * h + b + 1) * half)
            base = dot_nn(blended[...], proj_block(h, b))
            extra = dot_nn(low, up_ref[:, cols])
            for j in range(2):
                rs = slice(j * tokens, (j + 1) * tokens)
                gate = gate_ref[j : j + 1, cols]
                u = hidden_ref[rs, cols] + gate * base[rs]
                base_u[rs, cols] = u
                adj_u[rs, cols] = u + gate * extra[rs]

    def row_norm(u):
        return lax.rsqrt(jnp.mean(u * u, axis=-1, keepdims=True) + EPS)

    fgain = fgain_ref[...]
    for u_ref, vel_ref in ((base_u, base_vel), (adj_u, adj_vel)):
        u = u_ref[...]
        y = (u * row_norm(u) * fgain).astype(BF)
        vel_ref[...] = dot_nn(y, wout_ref[...])

    def tail_back(u, cotangent):
        dz = dot_nt(cotangent.astype(BF), wout_ref[...]) * fgain
        r = row_norm(u)
        z = u * r
        return r * (dz - z * jnp.mean(dz * z, axis=-1, keepdims=True))

    current = adjoint_ref[...]
    for j in range(2):
        rs = slice(j * tokens, (j + 1) * tokens)
        gate = gate_ref[j : j + 1, :]
        residual = coef_ref[j, 0] * (adj_vel[rs, :] - base_vel[rs, :]) + coef_ref[j, 1] * current
        adjusted = (tail_back(adj_u[rs, :], coef_ref[j, 2] * residual) * gate).astype(BF)
        adj_grad[rs, :] = adjusted
        low_grad[rs, :] = dot_nt(adjusted, up_ref[...]).astype(BF)

        hidden_grad = tail_back(base_u[rs, :], current)
        proj_grad = (hidden_grad * gate).astype(BF)
        blend_grad = jnp.zeros((tokens, inner), F32)
        for h in range(2):
            for b in range(2):
                cols = slice((2 * h + b) * half, (2 * h + b + 1) * half)
                blend_grad = blend_grad + dot_nt(proj_grad[:, cols], proj_block(h, b))
        blend_grad = blend_grad.astype(BF)

        normed_grad = jnp.zeros((tokens, width), F32)
        for h in range(2):
            dqs, dks, dvs = [], [], []
            for p in range(pairs):
                i = h * pairs + p
                db = split_heads(blend_grad[:, i * LANES : (i + 1) * LANES])
                a = att[i, j]
                da = dot_nt(db, vn[i, rs, :])
                ds = a * (da - jnp.sum(da * a, axis=-1, keepdims=True))
                ds = (ds * (1.0 / math.sqrt(HEAD_DIM))).astype(BF)
                dvs.append(dot_tn(a.astype(BF), db).astype(BF))
                dq2 = dot_nn(ds, kn[i, rs, :])
                dq = jnp.where(lane < HEAD_DIM, dq2[:tokens], dq2[tokens:])
                dk = dot_tn(ds, split_heads(qn[i, rs, :]))
                for grad, gain_ref, z_ref, r_ref, out in (
                    (dq, qgain_ref, qz, qr, dqs),
                    (dk, kgain_ref, kz, kr, dks),
                ):
                    dz = grad * gain_ref[...]
                    z = z_ref[i, rs, :]
                    out.append((r_ref[i, rs, :] * (dz - z * head_mean(dz * z))).astype(BF))
            for part, pieces in enumerate((dqs, dks, dvs)):
                grad = jnp.concatenate(pieces, axis=1)
                normed_grad = normed_grad + dot_nt(grad, qkv_block(h, part))

        hid = hidden_ref[rs, :]
        rh = row_norm(hid)
        hn = hid * rh
        dhn = normed_grad * scale1_ref[j : j + 1, :]
        total = hidden_grad + rh * (dhn - hn * jnp.mean(dhn * hn, axis=-1, keepdims=True))
        latent_grad = dot_nt(total.astype(BF), win_ref[...])
        current = current + (2.0 * latent_grad - current * coef_ref[j, 3]) * (1.0 / STEPS)

    adjoint_out_ref[...] = current
    down_out_ref[...] = dot_tn(blended[...], low_grad[...]).astype(BF)
    up_out_ref[...] = dot_tn(lowrank[...], adj_grad[...]).astype(BF)


def step_pair(core, coef, own, other, normed, hidden, adjoint, *rest):
    tokens, chan = adjoint.shape
    rows, width = hidden.shape
    shards, packed, half = own.shape
    inner, rank = rest[2].shape
    tiles = inner // LANES
    vmem = pl.BlockSpec(memory_space=pltpu.VMEM)
    smem = pl.BlockSpec(memory_space=pltpu.SMEM)
    hbm = pl.BlockSpec(memory_space=pl.ANY)
    f32_tiles = pltpu.VMEM((tiles, rows, LANES), F32)
    bf_tiles = pltpu.VMEM((tiles, rows, LANES), BF)
    return pl.pallas_call(
        step_pair_kernel,
        out_shape=(
            jax.ShapeDtypeStruct((tokens, chan), F32),
            jax.ShapeDtypeStruct((inner, rank), BF),
            jax.ShapeDtypeStruct((rank, width), BF),
        ),
        in_specs=[smem, smem, hbm, hbm] + [vmem] * (3 + len(rest)),
        out_specs=(vmem, vmem, vmem),
        scratch_shapes=[
            pltpu.VMEM((2, shards, packed, half), BF),
            pltpu.SemaphoreType.DMA((2,)),
            bf_tiles,
            f32_tiles,
            f32_tiles,
            bf_tiles,
            f32_tiles,
            f32_tiles,
            bf_tiles,
            pltpu.VMEM((tiles, 2, 2 * tokens, tokens), F32),
            pltpu.VMEM((rows, inner), BF),
            pltpu.VMEM((rows, width), F32),
            pltpu.VMEM((rows, width), F32),
            pltpu.VMEM((rows, chan), F32),
            pltpu.VMEM((rows, chan), F32),
            pltpu.VMEM((rows, rank), BF),
            pltpu.VMEM((rows, width), BF),
            pltpu.VMEM((rows, rank), BF),
        ],
        compiler_params=pltpu.CompilerParams(vmem_limit_bytes=50 * 1024 * 1024),
    )(core, coef, own, other, normed, hidden, adjoint, *rest)


def time_features(upper_time):
    halves = TIME_FEAT // 2
    frequency = jnp.exp(-math.log(10000.0) * jnp.arange(halves, dtype=F32) / halves)
    angles = 1000.0 * upper_time[..., None] * frequency
    return jnp.concatenate([jnp.cos(angles), jnp.sin(angles)], axis=-1).astype(BF)


def per_device(
    states,
    adjoint,
    grid_step_index,
    input_weight,
    timestep_weight,
    query_key_value_weight,
    projection_weight,
    down_factor,
    up_factor,
    query_norm_gain,
    key_norm_gain,
    final_norm_gain,
    output_weight,
):
    dp, shards = lax.axis_size("dp"), lax.axis_size("fsdp")
    sample_batch = dp * shards * states.shape[0]
    core = lax.axis_index("dp") % 2
    tokens, chan = states.shape[2:]
    width = input_weight.shape[1]
    inner = projection_weight.shape[1] // 2
    half = inner // 2
    rank = down_factor.shape[1]

    pieces = [
        lax.dynamic_slice_in_dim(query_key_value_weight, part * inner + core * half, half, 1)
        for part in range(3)
    ]
    pieces += [
        lax.dynamic_slice_in_dim(projection_weight, core * inner + b * half, half, 1)
        for b in range(2)
    ]
    own = lax.all_gather(jnp.concatenate(pieces, axis=0), "fsdp", axis=0)
    other = lax.ppermute(own, "dp", [(i, i ^ 1) for i in range(dp)])

    mod_cols = 3 * width // shards
    time_rows = timestep_weight.shape[0]
    n_time = time_rows * mod_cols // LANES
    n_down = down_factor.size // LANES
    n_up = up_factor.size // LANES

    def to_all(rows):
        return jnp.broadcast_to(rows[None], (shards,) + rows.shape)

    out = jnp.concatenate(
        [
            timestep_weight.reshape(time_rows, shards, mod_cols)
            .transpose(1, 0, 2)
            .reshape(shards, n_time, LANES),
            to_all(down_factor.reshape(n_down, LANES)),
            to_all(up_factor.reshape(n_up, LANES)),
            to_all(jnp.broadcast_to(grid_step_index.astype(BF)[:, None], (4, LANES))),
        ],
        axis=1,
    )
    got = lax.all_to_all(out, "fsdp", 0, 0, tiled=True)
    time_cols = got[:, :n_time].reshape(shards * time_rows, mod_cols)
    down_full = got[:, n_time : n_time + n_down].reshape(shards * down_factor.shape[0], rank)
    up_full = got[:, n_time + n_down : n_time + n_down + n_up].reshape(rank, width)
    steps = got[:, n_time + n_down + n_up, 0].astype(F32)

    turns = jnp.arange(2, dtype=F32)
    feats = time_features((steps[:, None] + 1.0 - turns) / STEPS)
    mods = jnp.dot(
        feats.reshape(2 * shards, TIME_FEAT), time_cols, preferred_element_type=F32
    ).reshape(shards, 2, mod_cols)
    mods = lax.all_to_all(mods, "fsdp", 0, 0, tiled=True)
    mods = mods.transpose(1, 0, 2).reshape(2, 3 * width)
    shift, scale1, gate = mods[:, :width], 1.0 + mods[:, width : 2 * width], mods[:, 2 * width :]

    hidden = jnp.dot(states[0].reshape(2 * tokens, chan), input_weight, preferred_element_type=F32)
    root = lax.rsqrt(jnp.mean(hidden * hidden, axis=-1, keepdims=True) + EPS)
    normed = (hidden * root).reshape(2, tokens, width) * scale1[:, None] + shift[:, None]
    normed = normed.astype(BF).reshape(2 * tokens, width)

    times = (grid_step_index[0].astype(F32) + 1.0 - turns) / STEPS
    sigma = jnp.sqrt(2.0 * (1.0 - times) / times)
    coef = jnp.stack([2.0 / sigma, sigma, 4.0 / (sigma * sample_batch), 1.0 / times], axis=1)

    adjoint_out, down_grad, up_grad = step_pair(
        core.astype(jnp.int32)[None],
        coef,
        own,
        other,
        normed,
        hidden,
        adjoint[0],
        scale1,
        gate,
        down_full,
        up_full,
        jnp.tile(query_norm_gain, 2)[None],
        jnp.tile(key_norm_gain, 2)[None],
        final_norm_gain[None],
        output_weight,
        input_weight,
    )

    out = jnp.concatenate(
        [down_grad.reshape(shards, n_down, LANES), up_grad.reshape(shards, n_up, LANES)], axis=1
    )
    got = lax.all_to_all(out, "fsdp", 0, 0, tiled=True)
    part = jnp.sum(got.astype(F32), axis=0).astype(BF)
    got = lax.all_to_all(
        jnp.broadcast_to(part[None], (dp,) + part.shape), "dp", 0, 0, tiled=True
    )
    part = jnp.sum(got.astype(F32), axis=0)
    return (
        adjoint_out[None],
        part[:n_down].reshape(down_factor.shape),
        part[n_down:].reshape(up_factor.shape),
    )


def solution(mesh):
    in_specs = (
        P(("dp", "fsdp"), None, None, None),
        P(("dp", "fsdp"), None, None),
        P(("dp", "fsdp")),
        P(),
        P("fsdp", None),
        P("fsdp", None),
        P("fsdp", None),
        P("fsdp", None),
        P("fsdp", None),
        P(),
        P(),
        P(),
        P(),
    )
    out_specs = (P(("dp", "fsdp"), None, None), P("fsdp", None), P("fsdp", None))
    return jax.shard_map(
        per_device, mesh=mesh, in_specs=in_specs, out_specs=out_specs, check_vma=False
    )
```

```python
import math

import jax
import jax.numpy as jnp
from jax import lax
from jax.experimental import pallas as pl
from jax.experimental.pallas import tpu as pltpu
from jax.sharding import PartitionSpec as P

HEAD_DIM = 64
TIME_FEAT = 256
STEPS = 28
LANES = 128
EPS = 1e-06
Y_CHIPS = 8
BF = jnp.bfloat16
F32 = jnp.float32


def dot_nn(a, b):
    return lax.dot_general(a, b, (((1,), (0,)), ((), ())), preferred_element_type=F32)


def dot_nt(a, b):
    return lax.dot_general(a, b, (((1,), (1,)), ((), ())), preferred_element_type=F32)


def dot_tn(a, b):
    return lax.dot_general(a, b, (((0,), (0,)), ((), ())), preferred_element_type=F32)


def step_pair_kernel(
    place_ref,
    coef_ref,
    *refs,
):
    (
        own_home,
        own_parts,
        other_home,
        other_parts,
        normed_ref,
        hidden_ref,
        adjoint_ref,
        scale1_ref,
        gate_ref,
        down_ref,
        up_ref,
        qgain_ref,
        kgain_ref,
        fgain_ref,
        wout_ref,
        win_ref,
        adjoint_out_ref,
        down_out_ref,
        up_out_ref,
        weights,
        sems,
        qn,
        qz,
        qr,
        kn,
        kz,
        kr,
        vn,
        att,
        blended,
        base_u,
        adj_u,
        base_vel,
        adj_vel,
        lowrank,
        adj_grad,
        low_grad,
    ) = (refs[0], refs[1:4], refs[4], refs[5:8]) + refs[8:]
    tokens = adjoint_ref.shape[0]
    rows = 2 * tokens
    width = hidden_ref.shape[1]
    _, _, shards, per_qkv, half = weights.shape
    inner = 2 * half
    per_proj = inner // shards
    pairs = half // LANES
    core, color = place_ref[0], place_ref[1]

    copies = []
    for side, home, parts in ((core, own_home, own_parts), (1 - core, other_home, other_parts)):
        copies.append((home.at[:, pl.ds(0, per_qkv), :], weights.at[side, color]))
        for n, part in enumerate(parts):
            piece = (color + jnp.where(side == 0, n + 1, 3 - n)) & 3
            copies.append((part, weights.at[side, piece]))
    copies = [
        pltpu.make_async_copy(source, target, sems.at[n])
        for n, (source, target) in enumerate(copies)
    ]
    for copy in copies:
        copy.start()

    lane = lax.broadcasted_iota(jnp.int32, (1, LANES), 1)
    even_f = (lane < HEAD_DIM).astype(F32)
    even = even_f.astype(BF)
    odd = (1.0 - even_f).astype(BF)
    row_i = lax.broadcasted_iota(jnp.int32, (2 * LANES, LANES), 0) & (LANES - 1)
    col_i = lax.broadcasted_iota(jnp.int32, (2 * LANES, LANES), 1)
    same = ((row_i >= HEAD_DIM) == (col_i >= HEAD_DIM)).astype(F32)
    averager = (same * (1.0 / HEAD_DIM)).astype(BF)

    def head_mean(values):
        high = values.astype(BF)
        low = (values - high.astype(F32)).astype(BF)
        return dot_nn(jnp.concatenate([high, low], axis=1), averager)

    def split_heads(tile):
        return jnp.concatenate([tile * even, tile * odd], axis=0)

    def qkv_block(h, part):
        return weights[h, part].reshape(width, half)

    def proj_block(h, b):
        return weights[h, 3, :, b * per_proj : (b + 1) * per_proj, :].reshape(inner, half)

    for copy in copies:
        copy.wait()

    normed = normed_ref[...]
    for h in range(2):
        for part, gain_ref, n_ref, z_ref, r_ref in (
            (0, qgain_ref, qn, qz, qr),
            (1, kgain_ref, kn, kz, kr),
        ):
            raw = dot_nn(normed, qkv_block(h, part))
            for p in range(pairs):
                x = raw[:, p * LANES : (p + 1) * LANES]
                r = lax.rsqrt(head_mean(x * x) + EPS)
                z = x * r
                z_ref[h * pairs + p] = z
                r_ref[h * pairs + p] = r
                n_ref[h * pairs + p] = (z * gain_ref[...]).astype(BF)
        raw = dot_nn(normed, qkv_block(h, 2)).astype(BF)
        for p in range(pairs):
            vn[h * pairs + p] = raw[:, p * LANES : (p + 1) * LANES]

    for i in range(2 * pairs):
        for j in range(2):
            rs = slice(j * tokens, (j + 1) * tokens)
            score = dot_nt(split_heads(qn[i, rs, :]), kn[i, rs, :]) * (1.0 / math.sqrt(HEAD_DIM))
            e = jnp.exp(score)
            a = e * (1.0 / jnp.sum(e, axis=-1, keepdims=True))
            att[i, j] = a
            ab = a.astype(BF)
            mixed = dot_nn(
                jnp.concatenate([ab[:tokens], ab[tokens:]], axis=1), split_heads(vn[i, rs, :])
            )
            blended[rs, i * LANES : (i + 1) * LANES] = mixed.astype(BF)

    low = dot_nn(blended[...], down_ref[...]).astype(BF)
    lowrank[...] = low
    for h in range(2):
        for b in range(2):
            cols = slice((2 * h + b) * half, (2 * h + b + 1) * half)
            base = dot_nn(blended[...], proj_block(h, b))
            extra = dot_nn(low, up_ref[:, cols])
            for j in range(2):
                rs = slice(j * tokens, (j + 1) * tokens)
                gate = gate_ref[j : j + 1, cols]
                u = hidden_ref[rs, cols] + gate * base[rs]
                base_u[rs, cols] = u
                adj_u[rs, cols] = u + gate * extra[rs]

    def row_norm(u):
        return lax.rsqrt(jnp.mean(u * u, axis=-1, keepdims=True) + EPS)

    fgain = fgain_ref[...]
    for u_ref, vel_ref in ((base_u, base_vel), (adj_u, adj_vel)):
        u = u_ref[...]
        y = (u * row_norm(u) * fgain).astype(BF)
        vel_ref[...] = dot_nn(y, wout_ref[...])

    def tail_back(u, cotangent):
        dz = dot_nt(cotangent.astype(BF), wout_ref[...]) * fgain
        r = row_norm(u)
        z = u * r
        return r * (dz - z * jnp.mean(dz * z, axis=-1, keepdims=True))

    current = adjoint_ref[...]
    for j in range(2):
        rs = slice(j * tokens, (j + 1) * tokens)
        gate = gate_ref[j : j + 1, :]
        residual = coef_ref[j, 0] * (adj_vel[rs, :] - base_vel[rs, :]) + coef_ref[j, 1] * current
        adjusted = (tail_back(adj_u[rs, :], coef_ref[j, 2] * residual) * gate).astype(BF)
        adj_grad[rs, :] = adjusted
        low_grad[rs, :] = dot_nt(adjusted, up_ref[...]).astype(BF)

        hidden_grad = tail_back(base_u[rs, :], current)
        proj_grad = (hidden_grad * gate).astype(BF)
        blend_grad = jnp.zeros((tokens, inner), F32)
        for h in range(2):
            for b in range(2):
                cols = slice((2 * h + b) * half, (2 * h + b + 1) * half)
                blend_grad = blend_grad + dot_nt(proj_grad[:, cols], proj_block(h, b))
        blend_grad = blend_grad.astype(BF)

        normed_grad = jnp.zeros((tokens, width), F32)
        for h in range(2):
            dqs, dks, dvs = [], [], []
            for p in range(pairs):
                i = h * pairs + p
                db = split_heads(blend_grad[:, i * LANES : (i + 1) * LANES])
                a = att[i, j]
                da = dot_nt(db, vn[i, rs, :])
                ds = a * (da - jnp.sum(da * a, axis=-1, keepdims=True))
                ds = (ds * (1.0 / math.sqrt(HEAD_DIM))).astype(BF)
                dvs.append(dot_tn(a.astype(BF), db).astype(BF))
                dq2 = dot_nn(ds, kn[i, rs, :])
                dq = jnp.where(lane < HEAD_DIM, dq2[:tokens], dq2[tokens:])
                dk = dot_tn(ds, split_heads(qn[i, rs, :]))
                for grad, gain_ref, z_ref, r_ref, out in (
                    (dq, qgain_ref, qz, qr, dqs),
                    (dk, kgain_ref, kz, kr, dks),
                ):
                    dz = grad * gain_ref[...]
                    z = z_ref[i, rs, :]
                    out.append((r_ref[i, rs, :] * (dz - z * head_mean(dz * z))).astype(BF))
            for part, pieces in enumerate((dqs, dks, dvs)):
                grad = jnp.concatenate(pieces, axis=1)
                normed_grad = normed_grad + dot_nt(grad, qkv_block(h, part))

        hid = hidden_ref[rs, :]
        rh = row_norm(hid)
        hn = hid * rh
        dhn = normed_grad * scale1_ref[j : j + 1, :]
        total = hidden_grad + rh * (dhn - hn * jnp.mean(dhn * hn, axis=-1, keepdims=True))
        latent_grad = dot_nt(total.astype(BF), win_ref[...])
        current = current + (2.0 * latent_grad - current * coef_ref[j, 3]) * (1.0 / STEPS)

    adjoint_out_ref[...] = current
    down_out_ref[...] = dot_tn(blended[...], low_grad[...]).astype(BF)
    up_out_ref[...] = dot_tn(lowrank[...], adj_grad[...]).astype(BF)


def step_pair(place, coef, gathered, normed, hidden, adjoint, *rest):
    tokens, chan = adjoint.shape
    rows, width = hidden.shape
    shards, packed, half = gathered[1].shape
    inner, rank = rest[2].shape
    tiles = inner // LANES
    vmem = pl.BlockSpec(memory_space=pltpu.VMEM)
    smem = pl.BlockSpec(memory_space=pltpu.SMEM)
    hbm = pl.BlockSpec(memory_space=pl.ANY)
    f32_tiles = pltpu.VMEM((tiles, rows, LANES), F32)
    bf_tiles = pltpu.VMEM((tiles, rows, LANES), BF)
    return pl.pallas_call(
        step_pair_kernel,
        out_shape=(
            jax.ShapeDtypeStruct((tokens, chan), F32),
            jax.ShapeDtypeStruct((inner, rank), BF),
            jax.ShapeDtypeStruct((rank, width), BF),
        ),
        in_specs=[smem, smem] + [hbm] * len(gathered) + [vmem] * (3 + len(rest)),
        out_specs=(vmem, vmem, vmem),
        scratch_shapes=[
            pltpu.VMEM((2, 4, shards, packed, half), BF),
            pltpu.SemaphoreType.DMA((len(gathered),)),
            bf_tiles,
            f32_tiles,
            f32_tiles,
            bf_tiles,
            f32_tiles,
            f32_tiles,
            bf_tiles,
            pltpu.VMEM((tiles, 2, 2 * tokens, tokens), F32),
            pltpu.VMEM((rows, inner), BF),
            pltpu.VMEM((rows, width), F32),
            pltpu.VMEM((rows, width), F32),
            pltpu.VMEM((rows, chan), F32),
            pltpu.VMEM((rows, chan), F32),
            pltpu.VMEM((rows, rank), BF),
            pltpu.VMEM((rows, width), BF),
            pltpu.VMEM((rows, rank), BF),
        ],
        compiler_params=pltpu.CompilerParams(vmem_limit_bytes=50 * 1024 * 1024),
    )(place, coef, *gathered, normed, hidden, adjoint, *rest)


def pieces_kernel(place_ref, qkv_ref, proj_ref, time_ref, extra_ref, out_ref):
    shards, _, half = out_ref.shape
    rows, per_proj = qkv_ref.shape[0], proj_ref.shape[0]
    time_rows, extra_rows = time_ref.shape[0], extra_ref.shape[0]
    owners = time_ref.shape[1] // half
    core, color = place_ref[0], place_ref[1]

    def columns(start):
        return pl.ds(pl.multiple_of(start, LANES), half)

    for r in range(shards):
        piece = (color + r // Y_CHIPS + 2 * (r % Y_CHIPS)) & 3

        @pl.when(piece < 3)
        def _():
            out_ref[r, 0:rows, :] = qkv_ref[:, columns((2 * piece + core) * half)]

        @pl.when(piece == 3)
        def _():
            for b in range(2):
                out_ref[r, b * per_proj : (b + 1) * per_proj, :] = proj_ref[
                    :, columns((2 * core + b) * half)
                ]

        owned = min(r, owners - 1)
        out_ref[r, rows : rows + time_rows, :] = time_ref[:, owned * half : (owned + 1) * half]
        out_ref[r, rows + time_rows : rows + time_rows + extra_rows, :] = extra_ref[...]


def pieces_for(place, qkv, proj, time, extra, shards):
    vmem = pl.BlockSpec(memory_space=pltpu.VMEM)
    rows = qkv.shape[0] + time.shape[0] + extra.shape[0]
    return pl.pallas_call(
        pieces_kernel,
        out_shape=jax.ShapeDtypeStruct((shards, rows, proj.shape[1] // 4), BF),
        in_specs=[pl.BlockSpec(memory_space=pltpu.SMEM)] + [vmem] * 4,
        out_specs=vmem,
    )(place, qkv, proj, time, extra)


def gather_weights(qkv, proj, time, extra, dp, shards):
    z_chips = dp // 4
    d, f = lax.axis_index("dp"), lax.axis_index("fsdp")
    core, z, x_hi = d % 2, (d // 2) % z_chips, d // (2 * z_chips)
    plane = 2 * x_hi + z
    color = (plane + f // Y_CHIPS + 2 * (f % Y_CHIPS)) % 4
    place = jnp.stack([core, plane]).astype(jnp.int32)
    home = lax.all_to_all(
        pieces_for(place, qkv, proj, time, extra, shards), "fsdp", 0, 0, tiled=True
    )

    def index(x, y, z, c):
        return ((x // 2 * z_chips + z) * 2 + c) * shards + (x % 2) * Y_CHIPS + y

    def neighbours(dx, dy, dz):
        return [
            (
                index((x + s * dx) % 4, (y + s * dy) % Y_CHIPS, (z + s * dz) % z_chips, c),
                index(x, y, z, c),
            )
            for x in range(4)
            for y in range(Y_CHIPS)
            for z in range(z_chips)
            for c, s in ((0, 1), (1, -1))
        ]

    piece = home[:, : qkv.shape[0]]
    parts = [
        lax.ppermute(piece, ("dp", "fsdp"), neighbours(*step))
        for step in ((1, 0, 0), (0, 1, 0), (0, 0, -1))
    ]
    own = [home] + parts
    swap = [(i, i ^ 1) for i in range(dp)]
    other = [lax.ppermute(block, "dp", swap) for block in own]
    return jnp.stack([core, color]).astype(jnp.int32), own + other


def time_features(upper_time):
    halves = TIME_FEAT // 2
    frequency = jnp.exp(-math.log(10000.0) * jnp.arange(halves, dtype=F32) / halves)
    angles = 1000.0 * upper_time[..., None] * frequency
    return jnp.concatenate([jnp.cos(angles), jnp.sin(angles)], axis=-1).astype(BF)


def per_device(
    states,
    adjoint,
    grid_step_index,
    input_weight,
    timestep_weight,
    query_key_value_weight,
    projection_weight,
    down_factor,
    up_factor,
    query_norm_gain,
    key_norm_gain,
    final_norm_gain,
    output_weight,
):
    dp, shards = lax.axis_size("dp"), lax.axis_size("fsdp")
    sample_batch = dp * shards * states.shape[0]
    core = lax.axis_index("dp") % 2
    tokens, chan = states.shape[2:]
    width = input_weight.shape[1]
    rank = down_factor.shape[1]

    half = projection_weight.shape[1] // 4
    rows, time_rows = query_key_value_weight.shape[0], timestep_weight.shape[0]
    n_up = up_factor.size // 2 // half
    n_down = down_factor.size // 2 // half
    n_step = -(n_up + n_down) % 8
    extra = jnp.concatenate(
        [
            lax.dynamic_slice_in_dim(up_factor.reshape(2 * n_up, half), core * n_up, n_up, 0),
            lax.dynamic_slice_in_dim(
                down_factor.reshape(2 * n_down, half), core * n_down, n_down, 0
            ),
            jnp.broadcast_to(grid_step_index.astype(BF)[:, None], (n_step, half)),
        ],
        axis=0,
    )
    place, gathered = gather_weights(
        query_key_value_weight, projection_weight, timestep_weight, extra, dp, shards
    )
    home, other_home = gathered[0], gathered[4]
    first = rows + time_rows

    def both(start, stop):
        mine, theirs = home[:, start:stop], other_home[:, start:stop]
        return jnp.stack(
            [jnp.where(core == 0, mine, theirs), jnp.where(core == 0, theirs, mine)], axis=1
        )

    up_full = both(first, first + n_up).reshape(rank, width)
    down_full = both(first + n_up, first + n_up + n_down).reshape(-1, rank)

    owners = 3 * width // half
    steps = home[:, first + n_up + n_down, 0].astype(F32)
    turns = jnp.arange(2, dtype=F32)
    feats = time_features((steps[:, None] + 1.0 - turns) / STEPS)
    mods = jnp.dot(
        feats.reshape(2 * shards, TIME_FEAT),
        home[:, rows:first].reshape(TIME_FEAT, half),
        preferred_element_type=F32,
    ).reshape(shards, 2, half)
    mods = lax.all_to_all(mods, "fsdp", 0, 0, tiled=True)[:owners]
    mods = mods.transpose(1, 0, 2).reshape(2, 3 * width)
    shift, scale1, gate = mods[:, :width], 1.0 + mods[:, width : 2 * width], mods[:, 2 * width :]

    hidden = jnp.dot(states[0].reshape(2 * tokens, chan), input_weight, preferred_element_type=F32)
    root = lax.rsqrt(jnp.mean(hidden * hidden, axis=-1, keepdims=True) + EPS)
    normed = (hidden * root).reshape(2, tokens, width) * scale1[:, None] + shift[:, None]
    normed = normed.astype(BF).reshape(2 * tokens, width)

    times = (grid_step_index[0].astype(F32) + 1.0 - turns) / STEPS
    sigma = jnp.sqrt(2.0 * (1.0 - times) / times)
    coef = jnp.stack([2.0 / sigma, sigma, 4.0 / (sigma * sample_batch), 1.0 / times], axis=1)

    adjoint_out, down_grad, up_grad = step_pair(
        place,
        coef,
        gathered,
        normed,
        hidden,
        adjoint[0],
        scale1,
        gate,
        down_full,
        up_full,
        jnp.tile(query_norm_gain, 2)[None],
        jnp.tile(key_norm_gain, 2)[None],
        final_norm_gain[None],
        output_weight,
        input_weight,
    )

    out = jnp.concatenate(
        [down_grad.reshape(shards, -1, LANES), up_grad.reshape(shards, -1, LANES)], axis=1
    )
    n_half = out.shape[1] // 2
    swap = [(i, i ^ 1) for i in range(dp)]
    keep = lax.dynamic_slice_in_dim(out, core * n_half, n_half, 1)
    give = lax.dynamic_slice_in_dim(out, (1 - core) * n_half, n_half, 1)
    out = (keep.astype(F32) + lax.ppermute(give, "dp", swap).astype(F32)).astype(BF)
    got = lax.all_to_all(out, "fsdp", 0, 0, tiled=True)
    part = jnp.sum(got.astype(F32), axis=0).astype(BF)
    chips = dp // 2
    got = lax.all_to_all(
        jnp.broadcast_to(part[None], (chips,) + part.shape),
        "dp",
        0,
        0,
        axis_index_groups=[[2 * i + c for i in range(chips)] for c in range(2)],
        tiled=True,
    )
    mine = jnp.sum(got.astype(F32), axis=0)
    theirs = lax.ppermute(mine, "dp", swap)
    part = jnp.concatenate(
        [jnp.where(core == 0, mine, theirs), jnp.where(core == 0, theirs, mine)], axis=0
    )
    return (
        adjoint_out[None],
        part[: down_factor.size // LANES].reshape(down_factor.shape),
        part[down_factor.size // LANES :].reshape(up_factor.shape),
    )


def solution(mesh):
    in_specs = (
        P(("dp", "fsdp"), None, None, None),
        P(("dp", "fsdp"), None, None),
        P(("dp", "fsdp")),
        P(),
        P("fsdp", None),
        P("fsdp", None),
        P("fsdp", None),
        P("fsdp", None),
        P("fsdp", None),
        P(),
        P(),
        P(),
        P(),
    )
    out_specs = (P(("dp", "fsdp"), None, None), P("fsdp", None), P("fsdp", None))
    return jax.shard_map(
        per_device, mesh=mesh, in_specs=in_specs, out_specs=out_specs, check_vma=False
    )
```

```python
from functools import partial
import math

import jax
import jax.numpy as jnp
from jax import lax
from jax.experimental import pallas as pl
from jax.experimental.pallas import tpu as pltpu
from jax.sharding import PartitionSpec as P

HEAD_DIM = 64
TIME_FEAT = 256
STEPS = 28
LANES = 128
EPS = 1e-06
Y_CHIPS = 8
BF = jnp.bfloat16
F32 = jnp.float32


def dot_nn(a, b):
    return lax.dot_general(a, b, (((1,), (0,)), ((), ())), preferred_element_type=F32)


def dot_nt(a, b):
    return lax.dot_general(a, b, (((1,), (1,)), ((), ())), preferred_element_type=F32)


def dot_tn(a, b):
    return lax.dot_general(a, b, (((0,), (0,)), ((), ())), preferred_element_type=F32)


def row_norm(u):
    return lax.rsqrt(jnp.mean(u * u, axis=-1, keepdims=True) + EPS)


def lane_index():
    return lax.broadcasted_iota(jnp.int32, (1, LANES), 1)


def split_heads(tile):
    even = (lane_index() < HEAD_DIM).astype(F32)
    return jnp.concatenate([tile * even.astype(BF), tile * (1.0 - even).astype(BF)], axis=0)


def head_averager():
    row = lax.broadcasted_iota(jnp.int32, (2 * LANES, LANES), 0) & (LANES - 1)
    col = lax.broadcasted_iota(jnp.int32, (2 * LANES, LANES), 1)
    same = ((row >= HEAD_DIM) == (col >= HEAD_DIM)).astype(F32)
    return (same * (1.0 / HEAD_DIM)).astype(BF)


def head_mean(values, averager):
    high = values.astype(BF)
    low = (values - high.astype(F32)).astype(BF)
    return dot_nn(jnp.concatenate([high, low], axis=1), averager)


def placement():
    z_chips = lax.axis_size("dp") // 4
    d, f = lax.axis_index("dp"), lax.axis_index("fsdp")
    core = lax.rem(d, 2)
    plane = 2 * lax.div(d, 2 * z_chips) + lax.rem(lax.div(d, 2), z_chips)
    return core, plane, (plane + lax.div(f, Y_CHIPS) + 2 * lax.rem(f, Y_CHIPS)) & 3


def load(sources, targets, sems):
    copies = [
        pltpu.make_async_copy(source, target, sems.at[n])
        for n, (source, target) in enumerate(zip(sources, targets, strict=True))
    ]
    for copy in copies:
        copy.start()
    return copies


def modulation(mods, j, which):
    width = mods.shape[1] // 3
    return mods[j : j + 1, which * width : (which + 1) * width]


def turn_time(step_ref, j):
    return (jnp.full((1, 1), step_ref[0], jnp.int32) + (1 - j)).astype(F32) / STEPS


def start_weights(gathered, weights, sems, pieces):
    core, _, color = placement()
    rows = pl.ds(0, weights.shape[3])
    for piece in pieces:
        for side, blocks in ((core, gathered[:4]), (1 - core, gathered[4:])):
            for n, block in enumerate(blocks):
                held = color if n == 0 else (color + jnp.where(side == 0, n, 4 - n)) & 3

                @pl.when(held == piece)
                def _():
                    pltpu.make_async_copy(
                        block.at[:, rows, :], weights.at[side, piece], sems.at[side, piece]
                    ).start()


def wait_weights(gathered, weights, sems, piece):
    for h in range(2):
        pltpu.make_async_copy(
            gathered[0].at[:, pl.ds(0, weights.shape[3]), :],
            weights.at[h, piece],
            sems.at[h, piece],
        ).wait()


def qkv_block(weights, part):
    half = weights.shape[4]
    return jnp.concatenate([weights[h, part].reshape(-1, half) for h in range(2)], axis=1)


def proj_block(weights, h):
    half, rows = weights.shape[4], weights.shape[3] // 2
    return jnp.concatenate(
        [weights[h, 3, :, b * rows : (b + 1) * rows, :].reshape(-1, half) for b in range(2)],
        axis=1,
    )


def tail_back(u, cotangent, wout_ref, fgain):
    dz = dot_nn(cotangent.astype(BF), wout_ref[...]) * fgain
    r = row_norm(u)
    z = u * r
    return r * (dz - z * jnp.mean(dz * z, axis=-1, keepdims=True))


def latent_step(
    current, decay, gate, scale1, hidden, wait, weights, base_u, att, norms, bits, gains, wout_ref,
    fgain, win_ref,
):
    tokens = current.shape[0]
    inner = weights.shape[4] * 2
    tiles = inner // LANES
    averager = head_averager()
    wait("base")
    hidden_grad = tail_back(base_u[...], current, wout_ref, fgain)
    proj_grad = (hidden_grad * gate).astype(BF)
    wait(3)
    blend_grad = jnp.zeros((tokens, inner), F32)
    for h in range(2):
        blend_grad = blend_grad + dot_nt(
            proj_grad[:, h * inner : (h + 1) * inner], proj_block(weights, h)
        )
    blend_grad = blend_grad.astype(BF)

    wait("state")
    grads = [[], [], []]
    for i in range(tiles):
        db = split_heads(blend_grad[:, i * LANES : (i + 1) * LANES])
        a = att[i]
        da = dot_nt(db, bits[2, i])
        ds = a * (da - jnp.sum(da * a, axis=-1, keepdims=True))
        ds = (ds * (1.0 / math.sqrt(HEAD_DIM))).astype(BF)
        grads[2].append(dot_tn(a.astype(BF), db).astype(BF))
        dq = dot_nn(ds, bits[1, i])
        dq = jnp.where(lane_index() < HEAD_DIM, dq[:tokens], dq[tokens:])
        dk = dot_tn(ds, split_heads(bits[0, i]))
        for n, grad in enumerate((dq, dk)):
            dz = grad * gains[n][...]
            z = norms[n, i]
            mean = head_mean(dz * z, averager)
            grads[n].append((norms[2 + n, i] * (dz - z * mean)).astype(BF))
    normed_grad = None
    for part in range(3):
        wait(part)
        term = dot_nt(jnp.concatenate(grads[part], axis=1), qkv_block(weights, part))
        normed_grad = term if normed_grad is None else normed_grad + term

    wait("hidden")
    hid = hidden[...]
    rh = row_norm(hid)
    hn = hid * rh
    dhn = normed_grad * scale1
    total = hidden_grad + rh * (dhn - hn * jnp.mean(dhn * hn, axis=-1, keepdims=True))
    latent_grad = dot_nt(total.astype(BF), win_ref[...])
    return current + (2.0 * latent_grad - current * decay) * (1.0 / STEPS)


def prepare_kernel(*refs):
    sources, outs = refs[:4], refs[4:8]
    blocks, hidden_ref, extra, in_sems = refs[8:12]
    up_wide, down_wide = refs[12:14]
    results, out_sems = refs[14:18], refs[18]
    normed, mods, up, down = results
    core, _, _ = placement()
    tokens, half = hidden_ref.shape[0] // 2, blocks.shape[2]
    extra_rows, shards = extra.shape[2], extra.shape[1]
    rows = pl.ds(sources[2].shape[1] - extra_rows, extra_rows)
    loads = load(
        [sources[0], sources[1], sources[2].at[:, rows, :], sources[3].at[:, rows, :]],
        [blocks, hidden_ref, extra.at[core], extra.at[1 - core]],
        in_sems,
    )

    for copy in loads[2:]:
        copy.wait()
    for h in range(2):
        for f in range(0, shards, 2):
            pair = [extra[h, f + n].astype(F32) for n in range(2)]
            for b in range(2):
                cols = slice((2 * h + b) * half, (2 * h + b + 1) * half)
                up_wide[4 * f : 4 * f + 8, cols] = jnp.concatenate(
                    [block[4 * b : 4 * b + 4] for block in pair], axis=0
                )
            for n in range(2):
                for k in range(3):
                    row = 48 * (f + n) + 24 * h + 8 * k
                    down_wide[row : row + 8, :] = pair[n][8:16, k * LANES : (k + 1) * LANES]
    up[...] = up_wide[...].astype(BF)
    down[...] = down_wide[:, 0 : down.shape[1]].astype(BF)

    for copy in loads[:2]:
        copy.wait()
    per = mods.shape[1] // 3 // half
    for o in range(3 * per):
        offset = 1.0 if o // per == 1 else 0.0
        mods[0:2, o * half : (o + 1) * half] = blocks[o] + offset
    for j in range(2):
        hid = hidden_ref[j * tokens : (j + 1) * tokens, :]
        scaled = hid * row_norm(hid) * modulation(mods, j, 1) + modulation(mods, j, 0)
        normed[j * tokens : (j + 1) * tokens, :] = scaled.astype(BF)
    for copy in load(results, outs, out_sems):
        copy.wait()


def prepare(blocks, hidden, home, other_home):
    rows, width = hidden.shape
    shards, _, half = home.shape
    inner, rank = 2 * half, HEAD_DIM
    results = [
        jax.ShapeDtypeStruct((rows, width), BF),
        jax.ShapeDtypeStruct((8, 3 * width), F32),
        jax.ShapeDtypeStruct((rank, width), BF),
        jax.ShapeDtypeStruct((inner, rank), BF),
    ]
    return pl.pallas_call(
        prepare_kernel,
        out_shape=results,
        in_specs=[HBM] * 4,
        out_specs=[HBM] * 4,
        scratch_shapes=like([blocks, hidden])
        + [
            pltpu.VMEM((2, shards, 16, half), BF),
            DMA((4,)),
            pltpu.VMEM((rank, width), F32),
            pltpu.VMEM((inner, LANES), F32),
        ]
        + like(results)
        + [DMA((4,))],
        compiler_params=pltpu.CompilerParams(vmem_limit_bytes=VMEM_LIMIT),
        cost_estimate=pl.CostEstimate(
            flops=5_000_000, bytes_accessed=8_000_000, transcendentals=0
        ),
    )(blocks, hidden, home, other_home)


def first_kernel(sample_batch, *refs):
    step_ref, gathered, refs = refs[0], refs[1:9], refs[9:]
    sources, refs = refs[:11], refs[11:]
    adjoint_out, packed_out, base_out, att_out, norms_out, bits_out = refs[:6]
    weights, sems, in_sems, out_sems = refs[6:10]
    targets, refs = refs[10:21], refs[21:]
    normed_ref, qgain_ref, kgain_ref, mods, hidden_ref, up_ref, down_ref, adjoint_ref, fgain_ref, wout_ref, win_ref = targets
    (
        base_u,
        att,
        norms,
        bits,
        blended,
        adj_u,
        adj_grad,
        low_grad,
        packed,
    ) = refs
    tokens = adjoint_ref.shape[1]
    inner = 2 * weights.shape[4]
    half = inner // 2
    tiles = inner // LANES
    shards = weights.shape[2]
    turns = [slice(j * tokens, (j + 1) * tokens) for j in range(2)]
    gains = (qgain_ref, kgain_ref)
    early = load(sources[:3], targets[:3], in_sems)
    start_weights(gathered, weights, sems, range(4))
    late = load(sources[3:], targets[3:], in_sems.at[pl.ds(3, 8)])

    def arrived(piece):
        wait_weights(gathered, weights, sems, piece)

    for copy in early:
        copy.wait()
    normed = normed_ref[...]
    averager = head_averager()
    for part in range(2):
        arrived(part)
        raw = dot_nn(normed, qkv_block(weights, part))
        for i in range(tiles):
            x = raw[:, i * LANES : (i + 1) * LANES]
            r = lax.rsqrt(head_mean(x * x, averager) + EPS)
            z = x * r
            n = (z * gains[part][...]).astype(BF)
            for j, rs in enumerate(turns):
                norms[j, part, i] = z[rs]
                norms[j, 2 + part, i] = r[rs]
                bits[j, part, i] = n[rs]
    arrived(2)
    raw = dot_nn(normed, qkv_block(weights, 2)).astype(BF)
    for i in range(tiles):
        for j, rs in enumerate(turns):
            bits[j, 2, i] = raw[rs, i * LANES : (i + 1) * LANES]

    for i in range(tiles):
        for j, rs in enumerate(turns):
            score = dot_nt(split_heads(bits[j, 0, i]), bits[j, 1, i]) * (1.0 / math.sqrt(HEAD_DIM))
            e = jnp.exp(score)
            a = e * (1.0 / jnp.sum(e, axis=-1, keepdims=True))
            att[j, i] = a
            ab = a.astype(BF)
            mixed = dot_nn(
                jnp.concatenate([ab[:tokens], ab[tokens:]], axis=1), split_heads(bits[j, 2, i])
            )
            blended[rs, i * LANES : (i + 1) * LANES] = mixed.astype(BF)

    for copy in late:
        copy.wait()
    fgain = fgain_ref[...]
    gates = [modulation(mods, j, 2) for j in range(2)]
    lowrank = dot_nn(blended[...], down_ref[...]).astype(BF)
    arrived(3)
    for h in range(2):
        cols = slice(h * inner, (h + 1) * inner)
        base = dot_nn(blended[...], proj_block(weights, h))
        extra = dot_nn(lowrank, up_ref[:, cols])
        for j, rs in enumerate(turns):
            gate = gates[j][:, cols]
            u = hidden_ref[rs, cols] + gate * base[rs]
            base_u[j, :, cols] = u
            adj_u[j, :, cols] = u + gate * extra[rs]

    outs = [
        pltpu.make_async_copy(source.at[1], target, out_sems.at[n])
        for n, (source, target) in enumerate(
            ((base_u, base_out), (att, att_out), (norms, norms_out), (bits, bits_out))
        )
    ]
    for copy in outs:
        copy.start()

    def velocity(u):
        return dot_nt((u * row_norm(u) * fgain).astype(BF), wout_ref[...])

    def regression(j, current):
        time = turn_time(step_ref, j)
        sigma = jnp.sqrt(2.0 * (1.0 - time) / time)
        gap = velocity(adj_u[j]) - velocity(base_u[j])
        residual = 2.0 / sigma * gap + sigma * current
        cotangent = 4.0 * residual / (sigma * sample_batch)
        grad = (tail_back(adj_u[j], cotangent, wout_ref, fgain) * gates[j]).astype(BF)
        adj_grad[turns[j], :] = grad
        low_grad[turns[j], :] = dot_nt(grad, up_ref[...]).astype(BF)

    current = adjoint_ref[...].T
    regression(0, current)
    current = latent_step(
        current,
        1.0 / turn_time(step_ref, 0),
        gates[0],
        modulation(mods, 0, 1),
        hidden_ref.at[turns[0], :],
        lambda what: None,
        weights,
        base_u.at[0],
        att.at[0],
        norms.at[0],
        bits.at[0],
        gains,
        wout_ref,
        fgain,
        win_ref,
    )
    regression(1, current)
    adjoint_out[...] = current

    down_grad = dot_tn(blended[...], low_grad[...])
    up_grad = dot_tn(lowrank, adj_grad[...])
    blank = jnp.zeros((8, LANES - down_grad.shape[1]), F32)
    for h in range(2):
        for f in range(shards):
            up_rows = jnp.concatenate(
                [
                    up_grad[4 * f : 4 * f + 4, (2 * h + b) * half : (2 * h + b + 1) * half]
                    for b in range(2)
                ],
                axis=0,
            )
            row = 48 * f + 24 * h
            down_rows = jnp.concatenate(
                [
                    jnp.concatenate([down_grad[row + 8 * k : row + 8 * k + 8], blank], axis=1)
                    for k in range(3)
                ],
                axis=1,
            )
            packed[h, f] = jnp.concatenate([up_rows, down_rows], axis=0).astype(BF)
    for copy in load([packed], [packed_out], in_sems):
        copy.wait()
    for copy in outs:
        copy.wait()


def second_kernel(*refs):
    step_ref, gathered, refs = refs[0], refs[1:9], refs[9:]
    sources, refs = refs[:12], refs[12:]
    adjoint_out, weights, sems, in_sems = refs[:4]
    targets = refs[4:]
    (
        base_u,
        adjoint_ref,
        mods,
        fgain_ref,
        wout_ref,
        att,
        norms,
        bits,
        qgain_ref,
        kgain_ref,
        hidden,
        win_ref,
    ) = targets
    tokens = adjoint_ref.shape[0]
    sources = list(sources)
    sources[10] = sources[10].at[pl.ds(tokens, tokens), :]
    loads = load(sources[:5], targets[:5], in_sems)
    start_weights(gathered, weights, sems, (3,))
    loads += load(sources[5:10], targets[5:10], in_sems.at[pl.ds(5, 5)])
    start_weights(gathered, weights, sems, range(3))
    loads += load(sources[10:], targets[10:], in_sems.at[pl.ds(10, 2)])
    for copy in loads[:5]:
        copy.wait()

    def wait(what):
        if what == "state":
            for copy in loads[5:10]:
                copy.wait()
        elif what == "hidden":
            for copy in loads[10:]:
                copy.wait()
        elif what != "base":
            wait_weights(gathered, weights, sems, what)

    result = latent_step(
        adjoint_ref[...],
        1.0 / turn_time(step_ref, 1),
        modulation(mods, 1, 2),
        modulation(mods, 1, 1),
        hidden,
        wait,
        weights,
        base_u,
        att,
        norms,
        bits,
        (qgain_ref, kgain_ref),
        wout_ref,
        fgain_ref[...],
        win_ref,
    )
    adjoint_out[...] = result.T


VMEM_LIMIT = 60 * 1024 * 1024


def state_shapes(tokens, width, inner):
    tiles = inner // LANES
    return (
        ((tokens, width), F32),
        ((tiles, 2 * tokens, tokens), F32),
        ((4, tiles, tokens, LANES), F32),
        ((3, tiles, tokens, LANES), BF),
    )


VMEM = pl.BlockSpec(memory_space=pltpu.VMEM)
SMEM = pl.BlockSpec(memory_space=pltpu.SMEM)
HBM = pl.BlockSpec(memory_space=pl.ANY)
DMA = pltpu.SemaphoreType.DMA


def like(arrays):
    return [pltpu.VMEM(a.shape, a.dtype) for a in arrays]


def step_pair_first(sample_batch, step, gathered, *rest):
    hidden, adjoint = rest[4], rest[7]
    chan, tokens = adjoint.shape
    rows, width = hidden.shape
    shards, _, half = gathered[0].shape
    per_qkv = width // shards
    inner, rank = 2 * half, HEAD_DIM
    state = state_shapes(tokens, width, inner)
    grads = (2, shards, 16, half)
    return pl.pallas_call(
        partial(first_kernel, sample_batch),
        out_shape=(jax.ShapeDtypeStruct((tokens, chan), F32), jax.ShapeDtypeStruct(grads, BF))
        + tuple(jax.ShapeDtypeStruct(*leaf) for leaf in state),
        in_specs=[SMEM] + [HBM] * (len(gathered) + len(rest)),
        out_specs=(VMEM, HBM) + (HBM,) * len(state),
        scratch_shapes=[
            pltpu.VMEM((2, 4, shards, per_qkv, half), BF),
            DMA((2, 4)),
            DMA((len(rest),)),
            DMA((len(state),)),
        ]
        + like(rest)
        + [pltpu.VMEM((2,) + shape, dtype) for shape, dtype in state]
        + [
            pltpu.VMEM((rows, inner), BF),
            pltpu.VMEM((2, tokens, width), F32),
            pltpu.VMEM((rows, width), BF),
            pltpu.VMEM((rows, rank), BF),
            pltpu.VMEM(grads, BF),
        ],
        compiler_params=pltpu.CompilerParams(vmem_limit_bytes=VMEM_LIMIT),
        cost_estimate=pl.CostEstimate(
            flops=5_000_000_000, bytes_accessed=20_000_000, transcendentals=400_000
        ),
    )(step, *gathered, *rest)


def step_pair_second(step, gathered, *rest):
    adjoint, hidden = rest[1], rest[10]
    tokens, chan = adjoint.shape
    width = hidden.shape[1]
    shards, _, half = gathered[0].shape
    scratch = like(rest)
    scratch[10] = pltpu.VMEM((tokens, width), F32)
    return pl.pallas_call(
        second_kernel,
        out_shape=jax.ShapeDtypeStruct((chan, tokens), F32),
        in_specs=[SMEM] + [HBM] * (len(gathered) + len(rest)),
        out_specs=VMEM,
        scratch_shapes=[
            pltpu.VMEM((2, 4, shards, width // shards, half), BF),
            DMA((2, 4)),
            DMA((len(rest),)),
        ]
        + scratch,
        compiler_params=pltpu.CompilerParams(vmem_limit_bytes=VMEM_LIMIT),
        cost_estimate=pl.CostEstimate(
            flops=3_000_000_000, bytes_accessed=20_000_000, transcendentals=0
        ),
    )(step, *gathered, *rest)


def pieces_kernel(step_ref, *refs):
    sources, out_ref = refs[:5], refs[5]
    targets, extra, out, in_sems, out_sems = refs[6:11], refs[11], refs[12], refs[13], refs[14]
    qkv_ref, proj_ref, time_ref, up_ref, down_ref = targets
    loads = load(sources, targets, in_sems)
    core, plane, _ = placement()
    shards, _, half = out.shape
    rows, per_proj, time_rows = qkv_ref.shape[0], proj_ref.shape[0], time_ref.shape[0]
    owners = time_ref.shape[1] // half
    first = rows + time_rows

    def columns(start):
        return pl.ds(pl.multiple_of(start, LANES), half)

    for copy in loads:
        copy.wait()
    for b in range(2):
        extra[4 * b : 4 * b + 4, :] = up_ref[:, columns((2 * core + b) * half)].astype(F32)
    extra[8:16, :] = jnp.full((8, half), step_ref[0], jnp.int32).astype(F32)
    down = down_ref[...].astype(F32)
    down = jnp.where(core == 0, down[:24], down[24:])
    for k in range(3):
        extra[8:16, k * LANES : k * LANES + down.shape[1]] = down[8 * k : 8 * k + 8]
    extra_bits = extra[...].astype(BF)

    copies = []
    for r in range(shards):
        piece = (plane + r // Y_CHIPS + 2 * (r % Y_CHIPS)) & 3

        @pl.when(piece < 3)
        def _():
            out[r, 0:rows, :] = qkv_ref[:, columns((2 * piece + core) * half)]

        @pl.when(piece == 3)
        def _():
            for b in range(2):
                out[r, b * per_proj : (b + 1) * per_proj, :] = proj_ref[
                    :, columns((2 * core + b) * half)
                ]

        owned = min(r, owners - 1)
        out[r, rows:first, :] = time_ref[:, owned * half : (owned + 1) * half]
        out[r, first : first + 16, :] = extra_bits
        copies.append(pltpu.make_async_copy(out.at[r], out_ref.at[r], out_sems.at[r]))
        copies[-1].start()
    for copy in copies:
        copy.wait()


def pieces_for(step, qkv, proj, time, up, down, shards):
    half = proj.shape[1] // 4
    shape = (shards, qkv.shape[0] + time.shape[0] + 16, half)
    inputs = (qkv, proj, time, up, down)
    return pl.pallas_call(
        pieces_kernel,
        out_shape=jax.ShapeDtypeStruct(shape, BF),
        in_specs=[SMEM] + [HBM] * len(inputs),
        out_specs=HBM,
        scratch_shapes=like(inputs)
        + [pltpu.VMEM((16, half), F32), pltpu.VMEM(shape, BF), DMA((len(inputs),)), DMA((shards,))],
        compiler_params=pltpu.CompilerParams(vmem_limit_bytes=VMEM_LIMIT),
    )(step, *inputs)


def gather_neighbours(home, mods, rows, dp, shards):
    z_chips = dp // 4

    def index(x, y, z, c):
        return ((x // 2 * z_chips + z) * 2 + c) * shards + (x % 2) * Y_CHIPS + y

    def neighbours(dx, dy, dz):
        return [
            (
                index((x + s * dx) % 4, (y + s * dy) % Y_CHIPS, (z + s * dz) % z_chips, c),
                index(x, y, z, c),
            )
            for x in range(4)
            for y in range(Y_CHIPS)
            for z in range(z_chips)
            for c, s in ((0, 1), (1, -1))
        ]

    swap = [(i, i ^ 1) for i in range(dp)]
    piece = home[:, :rows]
    parts = [
        lax.ppermute(piece, ("dp", "fsdp"), neighbours(*step))
        for step in ((0, 0, 1), (0, 1, 0), (-1, 0, 0))
    ]
    home, *parts[:2], mods = lax.optimization_barrier((home, *parts[:2], mods))
    own = [home] + parts
    return own + [lax.ppermute(block, "dp", swap) for block in own], mods


def time_features(upper_time):
    halves = TIME_FEAT // 2
    frequency = jnp.exp(-math.log(10000.0) * jnp.arange(halves, dtype=F32) / halves)
    angles = 1000.0 * upper_time[..., None] * frequency
    return jnp.concatenate([jnp.cos(angles), jnp.sin(angles)], axis=-1).astype(BF)


def per_device(
    states,
    adjoint,
    grid_step_index,
    input_weight,
    timestep_weight,
    query_key_value_weight,
    projection_weight,
    down_factor,
    up_factor,
    query_norm_gain,
    key_norm_gain,
    final_norm_gain,
    output_weight,
):
    dp, shards = lax.axis_size("dp"), lax.axis_size("fsdp")
    sample_batch = dp * shards * states.shape[0]
    core = lax.axis_index("dp") % 2
    tokens, chan = states.shape[2:]
    half = projection_weight.shape[1] // 4
    rows, time_rows = query_key_value_weight.shape[0], timestep_weight.shape[0]

    out = pieces_for(
        grid_step_index,
        query_key_value_weight,
        projection_weight,
        timestep_weight,
        up_factor,
        down_factor,
        shards,
    )
    home = lax.all_to_all(out, "fsdp", 0, 0, tiled=True)
    hidden = jnp.dot(states[0].reshape(2 * tokens, chan), input_weight, preferred_element_type=F32)
    gains = [jnp.tile(gain, 2)[None] for gain in (query_norm_gain, key_norm_gain)]
    fgain, wout = final_norm_gain[None], output_weight.T
    home, hidden, gains, fgain = lax.optimization_barrier((home, hidden, gains, fgain))

    steps = home[:, rows + time_rows + 8, HEAD_DIM].astype(F32)
    turns = jnp.arange(2, dtype=F32)
    feats = time_features((steps[:, None] + 1.0 - turns) / STEPS)
    mods = jnp.dot(
        feats.reshape(2 * shards, TIME_FEAT),
        home[:, rows : rows + time_rows].reshape(TIME_FEAT, half),
        preferred_element_type=F32,
    ).reshape(shards, 2, half)
    mods = lax.all_to_all(mods, "fsdp", 0, 0, tiled=True)
    gathered, mods = gather_neighbours(home, mods, rows, dp, shards)
    normed, mods, up_full, down_full = prepare(mods, hidden, home, gathered[4])

    adjoint_mid, out, base, att, norms, bits = step_pair_first(
        sample_batch,
        grid_step_index,
        gathered,
        normed,
        *gains,
        mods,
        hidden,
        up_full,
        down_full,
        adjoint[0].T,
        fgain,
        wout,
        input_weight,
    )

    swap = [(i, i ^ 1) for i in range(dp)]
    chips = dp // 2
    out = out.reshape((2 * shards,) + out.shape[2:])
    groups = [
        [(2 * i + c) * shards + f for c in range(2) for f in range(shards)] for i in range(chips)
    ]
    got = lax.all_to_all(out, ("dp", "fsdp"), 0, 0, axis_index_groups=groups, tiled=True)
    adjoint_out = step_pair_second(
        grid_step_index,
        gathered,
        base,
        adjoint_mid,
        mods,
        fgain,
        wout,
        att,
        norms,
        bits,
        *gains,
        hidden,
        input_weight,
    )
    got, adjoint_out = lax.optimization_barrier((got, adjoint_out))
    part = jnp.sum(got.astype(F32), axis=0).astype(BF)
    got = lax.all_to_all(
        jnp.broadcast_to(part[None], (chips,) + part.shape),
        "dp",
        0,
        0,
        axis_index_groups=[[2 * i + c for i in range(chips)] for c in range(2)],
        tiled=True,
    )
    mine = jnp.sum(got.astype(F32), axis=0)
    theirs = lax.ppermute(mine, "dp", swap)
    halves = [jnp.where(core == 0, mine, theirs), jnp.where(core == 0, theirs, mine)]
    down_grad = [
        block[8:, k * LANES : k * LANES + HEAD_DIM] for block in halves for k in range(3)
    ]
    up_grad = [block[4 * b : 4 * b + 4] for block in halves for b in range(2)]
    return (
        adjoint_out.T[None],
        jnp.concatenate(down_grad, axis=0),
        jnp.concatenate(up_grad, axis=1),
    )


def solution(mesh):
    in_specs = (
        P(("dp", "fsdp"), None, None, None),
        P(("dp", "fsdp"), None, None),
        P(("dp", "fsdp")),
        P(),
        P("fsdp", None),
        P("fsdp", None),
        P("fsdp", None),
        P("fsdp", None),
        P("fsdp", None),
        P(),
        P(),
        P(),
        P(),
    )
    out_specs = (P(("dp", "fsdp"), None, None), P("fsdp", None), P("fsdp", None))
    return jax.shard_map(
        per_device, mesh=mesh, in_specs=in_specs, out_specs=out_specs, check_vma=False
    )
```

```python
from functools import partial
import math

import jax
import jax.numpy as jnp
from jax import lax
from jax.experimental import pallas as pl
from jax.experimental.pallas import tpu as pltpu
from jax.sharding import PartitionSpec as P

HEAD_DIM = 64
TIME_FEAT = 256
STEPS = 28
LANES = 128
EPS = 1e-06
Y_CHIPS = 8
BF = jnp.bfloat16
F32 = jnp.float32


def dot_nn(a, b):
    return lax.dot_general(a, b, (((1,), (0,)), ((), ())), preferred_element_type=F32)


def dot_nt(a, b):
    return lax.dot_general(a, b, (((1,), (1,)), ((), ())), preferred_element_type=F32)


def dot_tn(a, b):
    return lax.dot_general(a, b, (((0,), (0,)), ((), ())), preferred_element_type=F32)


def row_norm(u):
    return lax.rsqrt(jnp.mean(u * u, axis=-1, keepdims=True) + EPS)


def lane_index():
    return lax.broadcasted_iota(jnp.int32, (1, LANES), 1)


def split_heads(tile):
    even = (lane_index() < HEAD_DIM).astype(F32)
    return jnp.concatenate([tile * even.astype(BF), tile * (1.0 - even).astype(BF)], axis=0)


def head_averager():
    row = lax.broadcasted_iota(jnp.int32, (2 * LANES, LANES), 0) & (LANES - 1)
    col = lax.broadcasted_iota(jnp.int32, (2 * LANES, LANES), 1)
    same = ((row >= HEAD_DIM) == (col >= HEAD_DIM)).astype(F32)
    return (same * (1.0 / HEAD_DIM)).astype(BF)


def head_mean(values, averager):
    high = values.astype(BF)
    low = (values - high.astype(F32)).astype(BF)
    return dot_nn(jnp.concatenate([high, low], axis=1), averager)


def placement():
    z_chips = lax.axis_size("dp") // 4
    d, f = lax.axis_index("dp"), lax.axis_index("fsdp")
    core = lax.rem(d, 2)
    plane = 2 * lax.div(d, 2 * z_chips) + lax.rem(lax.div(d, 2), z_chips)
    return core, plane, (plane + lax.div(f, Y_CHIPS) + 2 * lax.rem(f, Y_CHIPS)) & 3


def load(sources, targets, sems):
    copies = [
        pltpu.make_async_copy(source, target, sems.at[n])
        for n, (source, target) in enumerate(zip(sources, targets, strict=True))
    ]
    for copy in copies:
        copy.start()
    return copies


def modulation(mods, j, which):
    width = mods.shape[1] // 3
    return mods[j : j + 1, which * width : (which + 1) * width]


def turn_time(step_ref, j):
    return (jnp.full((1, 1), step_ref[0], jnp.int32) + (1 - j)).astype(F32) / STEPS


def start_weights(gathered, weights, sems, pieces):
    core, _, color = placement()
    rows = pl.ds(0, weights.shape[3])
    for piece in pieces:
        for side, blocks in ((core, gathered[:4]), (1 - core, gathered[4:])):
            for n, block in enumerate(blocks):
                held = color if n == 0 else (color + jnp.where(side == 0, n, 4 - n)) & 3

                @pl.when(held == piece)
                def _():
                    pltpu.make_async_copy(
                        block.at[:, rows, :], weights.at[side, piece], sems.at[side, piece]
                    ).start()


def wait_weights(gathered, weights, sems, piece):
    for h in range(2):
        pltpu.make_async_copy(
            gathered[0].at[:, pl.ds(0, weights.shape[3]), :],
            weights.at[h, piece],
            sems.at[h, piece],
        ).wait()


def qkv_block(weights, part):
    half = weights.shape[4]
    return jnp.concatenate([weights[h, part].reshape(-1, half) for h in range(2)], axis=1)


def proj_block(weights, h):
    half, rows = weights.shape[4], weights.shape[3] // 2
    return jnp.concatenate(
        [weights[h, 3, :, b * rows : (b + 1) * rows, :].reshape(-1, half) for b in range(2)],
        axis=1,
    )


def tail_back(u, cotangent, wout_ref, fgain):
    dz = dot_nn(cotangent.astype(BF), wout_ref[...]) * fgain
    r = row_norm(u)
    z = u * r
    return r * (dz - z * jnp.mean(dz * z, axis=-1, keepdims=True))


def latent_step(
    current, decay, gate, scale1, hidden, wait, weights, base_u, att, norms, bits, gains, wout_ref,
    fgain, win_ref,
):
    tokens = current.shape[0]
    inner = weights.shape[4] * 2
    tiles = inner // LANES
    averager = head_averager()
    wait("base")
    hidden_grad = tail_back(base_u[...], current, wout_ref, fgain)
    proj_grad = (hidden_grad * gate).astype(BF)
    wait(3)
    blend_grad = jnp.zeros((tokens, inner), F32)
    for h in range(2):
        blend_grad = blend_grad + dot_nt(
            proj_grad[:, h * inner : (h + 1) * inner], proj_block(weights, h)
        )
    blend_grad = blend_grad.astype(BF)

    wait("state")
    grads = [[], [], []]
    for i in range(tiles):
        db = split_heads(blend_grad[:, i * LANES : (i + 1) * LANES])
        a = att[i]
        da = dot_nt(db, bits[2, i])
        ds = a * (da - jnp.sum(da * a, axis=-1, keepdims=True))
        ds = (ds * (1.0 / math.sqrt(HEAD_DIM))).astype(BF)
        grads[2].append(dot_tn(a.astype(BF), db).astype(BF))
        dq = dot_nn(ds, bits[1, i])
        dq = jnp.where(lane_index() < HEAD_DIM, dq[:tokens], dq[tokens:])
        dk = dot_tn(ds, split_heads(bits[0, i]))
        for n, grad in enumerate((dq, dk)):
            dz = grad * gains[n][...]
            z = norms[n, i]
            mean = head_mean(dz * z, averager)
            grads[n].append((norms[2 + n, i] * (dz - z * mean)).astype(BF))
    normed_grad = None
    for part in range(3):
        wait(part)
        term = dot_nt(jnp.concatenate(grads[part], axis=1), qkv_block(weights, part))
        normed_grad = term if normed_grad is None else normed_grad + term

    wait("hidden")
    hid = hidden[...]
    rh = row_norm(hid)
    hn = hid * rh
    dhn = normed_grad * scale1
    total = hidden_grad + rh * (dhn - hn * jnp.mean(dhn * hn, axis=-1, keepdims=True))
    latent_grad = dot_nt(total.astype(BF), win_ref[...])
    return current + (2.0 * latent_grad - current * decay) * (1.0 / STEPS)


def first_kernel(sample_batch, *refs):
    step_ref, gathered, refs = refs[0], refs[1:9], refs[9:]
    sources, refs = refs[:8], refs[8:]
    adjoint_out, packed_out, base_out, att_out, norms_out, bits_out, mods_out = refs[:7]
    weights, sems, in_sems, extra_sems, out_sems = refs[7:12]
    targets, refs = refs[12:20], refs[20:]
    hidden_ref, blocks, qgain_ref, kgain_ref, adjoint_ref, fgain_ref, wout_ref, win_ref = targets
    (
        mods,
        extra,
        up_wide,
        up_ref,
        down_wide,
        down_ref,
        base_u,
        att,
        norms,
        bits,
        blended,
        adj_u,
        adj_grad,
        low_grad,
        packed,
    ) = refs
    tokens = adjoint_ref.shape[1]
    inner = 2 * weights.shape[4]
    half = inner // 2
    tiles = inner // LANES
    shards = weights.shape[2]
    turns = [slice(j * tokens, (j + 1) * tokens) for j in range(2)]
    gains = (qgain_ref, kgain_ref)
    core, _, _ = placement()
    early = load(sources[:4], targets[:4], in_sems)
    start_weights(gathered, weights, sems, range(4))
    extra_rows = pl.ds(gathered[0].shape[1] - extra.shape[2], extra.shape[2])
    late = load(
        [gathered[n].at[:, extra_rows, :] for n in (0, 4)],
        [extra.at[core], extra.at[1 - core]],
        extra_sems,
    )
    late += load(sources[4:], targets[4:], in_sems.at[pl.ds(4, 4)])

    def arrived(piece):
        wait_weights(gathered, weights, sems, piece)

    for copy in early:
        copy.wait()
    per = mods.shape[1] // 3 // half
    for o in range(3 * per):
        offset = 1.0 if o // per == 1 else 0.0
        mods[0:2, o * half : (o + 1) * half] = blocks[o] + offset
    normed = []
    for j, rs in enumerate(turns):
        hid = hidden_ref[rs, :]
        scaled = hid * row_norm(hid) * modulation(mods, j, 1) + modulation(mods, j, 0)
        normed.append(scaled.astype(BF))
    normed = jnp.concatenate(normed, axis=0)
    averager = head_averager()
    for part in range(2):
        arrived(part)
        raw = dot_nn(normed, qkv_block(weights, part))
        for i in range(tiles):
            x = raw[:, i * LANES : (i + 1) * LANES]
            r = lax.rsqrt(head_mean(x * x, averager) + EPS)
            z = x * r
            n = (z * gains[part][...]).astype(BF)
            for j, rs in enumerate(turns):
                norms[j, part, i] = z[rs]
                norms[j, 2 + part, i] = r[rs]
                bits[j, part, i] = n[rs]
    arrived(2)
    raw = dot_nn(normed, qkv_block(weights, 2)).astype(BF)
    for i in range(tiles):
        for j, rs in enumerate(turns):
            bits[j, 2, i] = raw[rs, i * LANES : (i + 1) * LANES]

    for i in range(tiles):
        for j, rs in enumerate(turns):
            score = dot_nt(split_heads(bits[j, 0, i]), bits[j, 1, i]) * (1.0 / math.sqrt(HEAD_DIM))
            e = jnp.exp(score)
            a = e * (1.0 / jnp.sum(e, axis=-1, keepdims=True))
            att[j, i] = a
            ab = a.astype(BF)
            mixed = dot_nn(
                jnp.concatenate([ab[:tokens], ab[tokens:]], axis=1), split_heads(bits[j, 2, i])
            )
            blended[rs, i * LANES : (i + 1) * LANES] = mixed.astype(BF)

    for copy in late:
        copy.wait()
    for h in range(2):
        for f in range(0, shards, 2):
            pair = [extra[h, f + n].astype(F32) for n in range(2)]
            for b in range(2):
                cols = slice((2 * h + b) * half, (2 * h + b + 1) * half)
                up_wide[4 * f : 4 * f + 8, cols] = jnp.concatenate(
                    [block[4 * b : 4 * b + 4] for block in pair], axis=0
                )
            for n in range(2):
                for k in range(3):
                    row = 48 * (f + n) + 24 * h + 8 * k
                    down_wide[row : row + 8, :] = pair[n][8:16, k * LANES : (k + 1) * LANES]
    up_ref[...] = up_wide[...].astype(BF)
    down_ref[...] = down_wide[:, 0 : down_ref.shape[1]].astype(BF)

    fgain = fgain_ref[...]
    gates = [modulation(mods, j, 2) for j in range(2)]
    lowrank = dot_nn(blended[...], down_ref[...]).astype(BF)
    arrived(3)
    for h in range(2):
        cols = slice(h * inner, (h + 1) * inner)
        base = dot_nn(blended[...], proj_block(weights, h))
        extra = dot_nn(lowrank, up_ref[:, cols])
        for j, rs in enumerate(turns):
            gate = gates[j][:, cols]
            u = hidden_ref[rs, cols] + gate * base[rs]
            base_u[j, :, cols] = u
            adj_u[j, :, cols] = u + gate * extra[rs]

    outs = [
        pltpu.make_async_copy(source.at[1], target, out_sems.at[n])
        for n, (source, target) in enumerate(
            ((base_u, base_out), (att, att_out), (norms, norms_out), (bits, bits_out))
        )
    ]
    outs.append(pltpu.make_async_copy(mods, mods_out, out_sems.at[4]))
    for copy in outs:
        copy.start()

    def velocity(u):
        return dot_nt((u * row_norm(u) * fgain).astype(BF), wout_ref[...])

    def regression(j, current):
        time = turn_time(step_ref, j)
        sigma = jnp.sqrt(2.0 * (1.0 - time) / time)
        gap = velocity(adj_u[j]) - velocity(base_u[j])
        residual = 2.0 / sigma * gap + sigma * current
        cotangent = 4.0 * residual / (sigma * sample_batch)
        grad = (tail_back(adj_u[j], cotangent, wout_ref, fgain) * gates[j]).astype(BF)
        adj_grad[turns[j], :] = grad
        low_grad[turns[j], :] = dot_nt(grad, up_ref[...]).astype(BF)

    current = adjoint_ref[...].T
    regression(0, current)
    current = latent_step(
        current,
        1.0 / turn_time(step_ref, 0),
        gates[0],
        modulation(mods, 0, 1),
        hidden_ref.at[turns[0], :],
        lambda what: None,
        weights,
        base_u.at[0],
        att.at[0],
        norms.at[0],
        bits.at[0],
        gains,
        wout_ref,
        fgain,
        win_ref,
    )
    regression(1, current)
    adjoint_out[...] = current

    down_grad = dot_tn(blended[...], low_grad[...])
    up_grad = dot_tn(lowrank, adj_grad[...])
    blank = jnp.zeros((8, LANES - down_grad.shape[1]), F32)
    for h in range(2):
        for f in range(shards):
            up_rows = jnp.concatenate(
                [
                    up_grad[4 * f : 4 * f + 4, (2 * h + b) * half : (2 * h + b + 1) * half]
                    for b in range(2)
                ],
                axis=0,
            )
            row = 48 * f + 24 * h
            down_rows = jnp.concatenate(
                [
                    jnp.concatenate([down_grad[row + 8 * k : row + 8 * k + 8], blank], axis=1)
                    for k in range(3)
                ],
                axis=1,
            )
            packed[h, f] = jnp.concatenate([up_rows, down_rows], axis=0).astype(BF)
    for copy in load([packed], [packed_out], in_sems):
        copy.wait()
    for copy in outs:
        copy.wait()


def second_kernel(*refs):
    step_ref, gathered, refs = refs[0], refs[1:9], refs[9:]
    sources, refs = refs[:12], refs[12:]
    adjoint_out, weights, sems, in_sems = refs[:4]
    targets = refs[4:]
    (
        base_u,
        adjoint_ref,
        mods,
        fgain_ref,
        wout_ref,
        att,
        norms,
        bits,
        qgain_ref,
        kgain_ref,
        hidden,
        win_ref,
    ) = targets
    tokens = adjoint_ref.shape[0]
    sources = list(sources)
    sources[10] = sources[10].at[pl.ds(tokens, tokens), :]
    loads = load(sources[:5], targets[:5], in_sems)
    start_weights(gathered, weights, sems, (3,))
    loads += load(sources[5:10], targets[5:10], in_sems.at[pl.ds(5, 5)])
    start_weights(gathered, weights, sems, range(3))
    loads += load(sources[10:], targets[10:], in_sems.at[pl.ds(10, 2)])
    for copy in loads[:5]:
        copy.wait()

    def wait(what):
        if what == "state":
            for copy in loads[5:10]:
                copy.wait()
        elif what == "hidden":
            for copy in loads[10:]:
                copy.wait()
        elif what != "base":
            wait_weights(gathered, weights, sems, what)

    result = latent_step(
        adjoint_ref[...],
        1.0 / turn_time(step_ref, 1),
        modulation(mods, 1, 2),
        modulation(mods, 1, 1),
        hidden,
        wait,
        weights,
        base_u,
        att,
        norms,
        bits,
        (qgain_ref, kgain_ref),
        wout_ref,
        fgain_ref[...],
        win_ref,
    )
    adjoint_out[...] = result.T


VMEM_LIMIT = 60 * 1024 * 1024


def state_shapes(tokens, width, inner):
    tiles = inner // LANES
    return (
        ((tokens, width), F32),
        ((tiles, 2 * tokens, tokens), F32),
        ((4, tiles, tokens, LANES), F32),
        ((3, tiles, tokens, LANES), BF),
    )


VMEM = pl.BlockSpec(memory_space=pltpu.VMEM)
SMEM = pl.BlockSpec(memory_space=pltpu.SMEM)
HBM = pl.BlockSpec(memory_space=pl.ANY)
DMA = pltpu.SemaphoreType.DMA


def like(arrays):
    return [pltpu.VMEM(a.shape, a.dtype) for a in arrays]


def step_pair_first(sample_batch, step, gathered, *rest):
    hidden, adjoint = rest[0], rest[4]
    chan, tokens = adjoint.shape
    rows, width = hidden.shape
    shards, _, half = gathered[0].shape
    per_qkv = width // shards
    inner, rank = 2 * half, HEAD_DIM
    state = state_shapes(tokens, width, inner)
    grads = (2, shards, 16, half)
    mods = (8, 3 * width)
    return pl.pallas_call(
        partial(first_kernel, sample_batch),
        out_shape=(jax.ShapeDtypeStruct((tokens, chan), F32), jax.ShapeDtypeStruct(grads, BF))
        + tuple(jax.ShapeDtypeStruct(*leaf) for leaf in state)
        + (jax.ShapeDtypeStruct(mods, F32),),
        in_specs=[SMEM] + [HBM] * (len(gathered) + len(rest)),
        out_specs=(VMEM, HBM) + (HBM,) * (len(state) + 1),
        scratch_shapes=[
            pltpu.VMEM((2, 4, shards, per_qkv, half), BF),
            DMA((2, 4)),
            DMA((len(rest),)),
            DMA((2,)),
            DMA((len(state) + 1,)),
        ]
        + like(rest)
        + [
            pltpu.VMEM(mods, F32),
            pltpu.VMEM(grads, BF),
            pltpu.VMEM((rank, width), F32),
            pltpu.VMEM((rank, width), BF),
            pltpu.VMEM((inner, LANES), F32),
            pltpu.VMEM((inner, rank), BF),
        ]
        + [pltpu.VMEM((2,) + shape, dtype) for shape, dtype in state]
        + [
            pltpu.VMEM((rows, inner), BF),
            pltpu.VMEM((2, tokens, width), F32),
            pltpu.VMEM((rows, width), BF),
            pltpu.VMEM((rows, rank), BF),
            pltpu.VMEM(grads, BF),
        ],
        compiler_params=pltpu.CompilerParams(vmem_limit_bytes=VMEM_LIMIT),
        cost_estimate=pl.CostEstimate(
            flops=5_000_000_000, bytes_accessed=20_000_000, transcendentals=400_000
        ),
    )(step, *gathered, *rest)


def step_pair_second(step, gathered, *rest):
    adjoint, hidden = rest[1], rest[10]
    tokens, chan = adjoint.shape
    width = hidden.shape[1]
    shards, _, half = gathered[0].shape
    scratch = like(rest)
    scratch[10] = pltpu.VMEM((tokens, width), F32)
    return pl.pallas_call(
        second_kernel,
        out_shape=jax.ShapeDtypeStruct((chan, tokens), F32),
        in_specs=[SMEM] + [HBM] * (len(gathered) + len(rest)),
        out_specs=VMEM,
        scratch_shapes=[
            pltpu.VMEM((2, 4, shards, width // shards, half), BF),
            DMA((2, 4)),
            DMA((len(rest),)),
        ]
        + scratch,
        compiler_params=pltpu.CompilerParams(vmem_limit_bytes=VMEM_LIMIT),
        cost_estimate=pl.CostEstimate(
            flops=3_000_000_000, bytes_accessed=20_000_000, transcendentals=0
        ),
    )(step, *gathered, *rest)


def pieces_kernel(step_ref, *refs):
    sources, out_ref = refs[:5], refs[5]
    targets, extra, out, in_sems, out_sems = refs[6:11], refs[11], refs[12], refs[13], refs[14]
    qkv_ref, proj_ref, time_ref, up_ref, down_ref = targets
    loads = load(sources, targets, in_sems)
    core, plane, _ = placement()
    shards, _, half = out.shape
    rows, per_proj, time_rows = qkv_ref.shape[0], proj_ref.shape[0], time_ref.shape[0]
    owners = time_ref.shape[1] // half
    first = rows + time_rows

    def columns(start):
        return pl.ds(pl.multiple_of(start, LANES), half)

    for copy in loads:
        copy.wait()
    for b in range(2):
        extra[4 * b : 4 * b + 4, :] = up_ref[:, columns((2 * core + b) * half)].astype(F32)
    extra[8:16, :] = jnp.full((8, half), step_ref[0], jnp.int32).astype(F32)
    down = down_ref[...].astype(F32)
    down = jnp.where(core == 0, down[:24], down[24:])
    for k in range(3):
        extra[8:16, k * LANES : k * LANES + down.shape[1]] = down[8 * k : 8 * k + 8]
    extra_bits = extra[...].astype(BF)

    copies = []
    for r in range(shards):
        piece = (plane + r // Y_CHIPS + 2 * (r % Y_CHIPS)) & 3

        @pl.when(piece < 3)
        def _():
            out[r, 0:rows, :] = qkv_ref[:, columns((2 * piece + core) * half)]

        @pl.when(piece == 3)
        def _():
            for b in range(2):
                out[r, b * per_proj : (b + 1) * per_proj, :] = proj_ref[
                    :, columns((2 * core + b) * half)
                ]

        owned = min(r, owners - 1)
        out[r, rows:first, :] = time_ref[:, owned * half : (owned + 1) * half]
        out[r, first : first + 16, :] = extra_bits
        copies.append(pltpu.make_async_copy(out.at[r], out_ref.at[r], out_sems.at[r]))
        copies[-1].start()
    for copy in copies:
        copy.wait()


def pieces_for(step, qkv, proj, time, up, down, shards):
    half = proj.shape[1] // 4
    shape = (shards, qkv.shape[0] + time.shape[0] + 16, half)
    inputs = (qkv, proj, time, up, down)
    return pl.pallas_call(
        pieces_kernel,
        out_shape=jax.ShapeDtypeStruct(shape, BF),
        in_specs=[SMEM] + [HBM] * len(inputs),
        out_specs=HBM,
        scratch_shapes=like(inputs)
        + [pltpu.VMEM((16, half), F32), pltpu.VMEM(shape, BF), DMA((len(inputs),)), DMA((shards,))],
        compiler_params=pltpu.CompilerParams(vmem_limit_bytes=VMEM_LIMIT),
    )(step, *inputs)


def gather_neighbours(home, mods, rows, dp, shards):
    z_chips = dp // 4

    def index(x, y, z, c):
        return ((x // 2 * z_chips + z) * 2 + c) * shards + (x % 2) * Y_CHIPS + y

    def neighbours(dx, dy, dz):
        return [
            (
                index((x + s * dx) % 4, (y + s * dy) % Y_CHIPS, (z + s * dz) % z_chips, c),
                index(x, y, z, c),
            )
            for x in range(4)
            for y in range(Y_CHIPS)
            for z in range(z_chips)
            for c, s in ((0, 1), (1, -1))
        ]

    swap = [(i, i ^ 1) for i in range(dp)]
    piece = home[:, :rows]
    parts = [
        lax.ppermute(piece, ("dp", "fsdp"), neighbours(*step))
        for step in ((0, 0, 1), (0, 1, 0), (-1, 0, 0))
    ]
    home, *parts[:2], mods = lax.optimization_barrier((home, *parts[:2], mods))
    own = [home] + parts
    return own + [lax.ppermute(block, "dp", swap) for block in own], mods


def time_features(upper_time):
    halves = TIME_FEAT // 2
    frequency = jnp.exp(-math.log(10000.0) * jnp.arange(halves, dtype=F32) / halves)
    angles = 1000.0 * upper_time[..., None] * frequency
    return jnp.concatenate([jnp.cos(angles), jnp.sin(angles)], axis=-1).astype(BF)


def per_device(
    states,
    adjoint,
    grid_step_index,
    input_weight,
    timestep_weight,
    query_key_value_weight,
    projection_weight,
    down_factor,
    up_factor,
    query_norm_gain,
    key_norm_gain,
    final_norm_gain,
    output_weight,
):
    dp, shards = lax.axis_size("dp"), lax.axis_size("fsdp")
    sample_batch = dp * shards * states.shape[0]
    core = lax.axis_index("dp") % 2
    tokens, chan = states.shape[2:]
    half = projection_weight.shape[1] // 4
    rows, time_rows = query_key_value_weight.shape[0], timestep_weight.shape[0]

    out = pieces_for(
        grid_step_index,
        query_key_value_weight,
        projection_weight,
        timestep_weight,
        up_factor,
        down_factor,
        shards,
    )
    home = lax.all_to_all(out, "fsdp", 0, 0, tiled=True)
    hidden = jnp.dot(states[0].reshape(2 * tokens, chan), input_weight, preferred_element_type=F32)
    gains = [jnp.tile(gain, 2)[None] for gain in (query_norm_gain, key_norm_gain)]
    fgain, wout = final_norm_gain[None], output_weight.T
    home, hidden, gains, fgain = lax.optimization_barrier((home, hidden, gains, fgain))

    steps = home[:, rows + time_rows + 8, HEAD_DIM].astype(F32)
    turns = jnp.arange(2, dtype=F32)
    feats = time_features((steps[:, None] + 1.0 - turns) / STEPS)
    mods = jnp.dot(
        feats.reshape(2 * shards, TIME_FEAT),
        home[:, rows : rows + time_rows].reshape(TIME_FEAT, half),
        preferred_element_type=F32,
    ).reshape(shards, 2, half)
    mods = lax.all_to_all(mods, "fsdp", 0, 0, tiled=True)
    gathered, mods = gather_neighbours(home, mods, rows, dp, shards)

    adjoint_mid, out, base, att, norms, bits, mods = step_pair_first(
        sample_batch,
        grid_step_index,
        gathered,
        hidden,
        mods,
        *gains,
        adjoint[0].T,
        fgain,
        wout,
        input_weight,
    )

    swap = [(i, i ^ 1) for i in range(dp)]
    chips = dp // 2
    out = out.reshape((2 * shards,) + out.shape[2:])
    groups = [
        [(2 * i + c) * shards + f for c in range(2) for f in range(shards)] for i in range(chips)
    ]
    got = lax.all_to_all(out, ("dp", "fsdp"), 0, 0, axis_index_groups=groups, tiled=True)
    adjoint_out = step_pair_second(
        grid_step_index,
        gathered,
        base,
        adjoint_mid,
        mods,
        fgain,
        wout,
        att,
        norms,
        bits,
        *gains,
        hidden,
        input_weight,
    )
    got, adjoint_out = lax.optimization_barrier((got, adjoint_out))
    part = jnp.sum(got.astype(F32), axis=0).astype(BF)
    got = lax.all_to_all(
        jnp.broadcast_to(part[None], (chips,) + part.shape),
        "dp",
        0,
        0,
        axis_index_groups=[[2 * i + c for i in range(chips)] for c in range(2)],
        tiled=True,
    )
    mine = jnp.sum(got.astype(F32), axis=0)
    theirs = lax.ppermute(mine, "dp", swap)
    halves = [jnp.where(core == 0, mine, theirs), jnp.where(core == 0, theirs, mine)]
    down_grad = [
        block[8:, k * LANES : k * LANES + HEAD_DIM] for block in halves for k in range(3)
    ]
    up_grad = [block[4 * b : 4 * b + 4] for block in halves for b in range(2)]
    return (
        adjoint_out.T[None],
        jnp.concatenate(down_grad, axis=0),
        jnp.concatenate(up_grad, axis=1),
    )


def solution(mesh):
    in_specs = (
        P(("dp", "fsdp"), None, None, None),
        P(("dp", "fsdp"), None, None),
        P(("dp", "fsdp")),
        P(),
        P("fsdp", None),
        P("fsdp", None),
        P("fsdp", None),
        P("fsdp", None),
        P("fsdp", None),
        P(),
        P(),
        P(),
        P(),
    )
    out_specs = (P(("dp", "fsdp"), None, None), P("fsdp", None), P("fsdp", None))
    return jax.shard_map(
        per_device, mesh=mesh, in_specs=in_specs, out_specs=out_specs, check_vma=False
    )
```

```python
from functools import partial
import math

import jax
import jax.numpy as jnp
from jax import lax
from jax.experimental import pallas as pl
from jax.experimental.pallas import tpu as pltpu
from jax.sharding import PartitionSpec as P

HEAD_DIM = 64
TIME_FEAT = 256
STEPS = 28
LANES = 128
EPS = 1e-06
Y_CHIPS = 8
BF = jnp.bfloat16
F32 = jnp.float32


def dot_nn(a, b):
    return lax.dot_general(a, b, (((1,), (0,)), ((), ())), preferred_element_type=F32)


def dot_nt(a, b):
    return lax.dot_general(a, b, (((1,), (1,)), ((), ())), preferred_element_type=F32)


def dot_tn(a, b):
    return lax.dot_general(a, b, (((0,), (0,)), ((), ())), preferred_element_type=F32)


def row_norm(u):
    return lax.rsqrt(jnp.mean(u * u, axis=-1, keepdims=True) + EPS)


def lane_index():
    return lax.broadcasted_iota(jnp.int32, (1, LANES), 1)


def split_heads(tile):
    even = (lane_index() < HEAD_DIM).astype(F32)
    return jnp.concatenate([tile * even.astype(BF), tile * (1.0 - even).astype(BF)], axis=0)


def head_averager():
    row = lax.broadcasted_iota(jnp.int32, (2 * LANES, LANES), 0) & (LANES - 1)
    col = lax.broadcasted_iota(jnp.int32, (2 * LANES, LANES), 1)
    same = ((row >= HEAD_DIM) == (col >= HEAD_DIM)).astype(F32)
    return (same * (1.0 / HEAD_DIM)).astype(BF)


def head_mean(values, averager):
    high = values.astype(BF)
    low = (values - high.astype(F32)).astype(BF)
    return dot_nn(jnp.concatenate([high, low], axis=1), averager)


def placement():
    z_chips = lax.axis_size("dp") // 4
    d, f = lax.axis_index("dp"), lax.axis_index("fsdp")
    core = lax.rem(d, 2)
    plane = 2 * lax.div(d, 2 * z_chips) + lax.rem(lax.div(d, 2), z_chips)
    return core, plane, (plane + lax.div(f, Y_CHIPS) + 2 * lax.rem(f, Y_CHIPS)) & 3


def load(sources, targets, sems):
    copies = [
        pltpu.make_async_copy(source, target, sems.at[n])
        for n, (source, target) in enumerate(zip(sources, targets, strict=True))
    ]
    for copy in copies:
        copy.start()
    return copies


def modulation(mods, j, which):
    width = mods.shape[1] // 3
    return mods[j : j + 1, which * width : (which + 1) * width]


def turn_time(step_ref, j):
    return (jnp.full((1, 1), step_ref[0], jnp.int32) + (1 - j)).astype(F32) / STEPS


def start_weights(gathered, weights, sems, pieces):
    core, _, color = placement()
    rows = pl.ds(0, weights.shape[3])
    for piece in pieces:
        for side, blocks in ((core, gathered[:4]), (1 - core, gathered[4:])):
            for n, block in enumerate(blocks):
                held = color if n == 0 else (color + jnp.where(side == 0, n, 4 - n)) & 3

                @pl.when(held == piece)
                def _():
                    pltpu.make_async_copy(
                        block.at[:, rows, :], weights.at[side, piece], sems.at[side, piece]
                    ).start()


def wait_weights(gathered, weights, sems, piece):
    for h in range(2):
        pltpu.make_async_copy(
            gathered[0].at[:, pl.ds(0, weights.shape[3]), :],
            weights.at[h, piece],
            sems.at[h, piece],
        ).wait()


def qkv_block(weights, part):
    half = weights.shape[4]
    return jnp.concatenate([weights[h, part].reshape(-1, half) for h in range(2)], axis=1)


def proj_block(weights, h):
    half, rows = weights.shape[4], weights.shape[3] // 2
    return jnp.concatenate(
        [weights[h, 3, :, b * rows : (b + 1) * rows, :].reshape(-1, half) for b in range(2)],
        axis=1,
    )


def tail_back(u, cotangent, wout_ref, fgain):
    dz = dot_nn(cotangent.astype(BF), wout_ref[...]) * fgain
    r = row_norm(u)
    z = u * r
    return r * (dz - z * jnp.mean(dz * z, axis=-1, keepdims=True))


def latent_step(
    current, decay, gate, scale1, hidden, wait, weights, base_u, att, norms, bits, gains, wout_ref,
    fgain, win_ref,
):
    tokens = current.shape[0]
    inner = weights.shape[4] * 2
    tiles = inner // LANES
    averager = head_averager()
    wait("base")
    hidden_grad = tail_back(base_u[...], current, wout_ref, fgain)
    proj_grad = (hidden_grad * gate).astype(BF)
    wait(3)
    blend_grad = jnp.zeros((tokens, inner), F32)
    for h in range(2):
        blend_grad = blend_grad + dot_nt(
            proj_grad[:, h * inner : (h + 1) * inner], proj_block(weights, h)
        )
    blend_grad = blend_grad.astype(BF)

    wait("state")
    grads = [[], [], []]
    for i in range(tiles):
        db = split_heads(blend_grad[:, i * LANES : (i + 1) * LANES])
        a = att[i]
        da = dot_nt(db, bits[2, i])
        ds = a * (da - jnp.sum(da * a, axis=-1, keepdims=True))
        ds = (ds * (1.0 / math.sqrt(HEAD_DIM))).astype(BF)
        grads[2].append(dot_tn(a.astype(BF), db).astype(BF))
        dq = dot_nn(ds, bits[1, i])
        dq = jnp.where(lane_index() < HEAD_DIM, dq[:tokens], dq[tokens:])
        dk = dot_tn(ds, split_heads(bits[0, i]))
        for n, grad in enumerate((dq, dk)):
            dz = grad * gains[n][...]
            z = norms[n, i]
            mean = head_mean(dz * z, averager)
            grads[n].append((norms[2 + n, i] * (dz - z * mean)).astype(BF))
    normed_grad = None
    for part in range(3):
        wait(part)
        term = dot_nt(jnp.concatenate(grads[part], axis=1), qkv_block(weights, part))
        normed_grad = term if normed_grad is None else normed_grad + term

    wait("hidden")
    hid = hidden[...]
    rh = row_norm(hid)
    hn = hid * rh
    dhn = normed_grad * scale1
    total = hidden_grad + rh * (dhn - hn * jnp.mean(dhn * hn, axis=-1, keepdims=True))
    latent_grad = dot_nt(total.astype(BF), win_ref[...])
    return current + (2.0 * latent_grad - current * decay) * (1.0 / STEPS)


def first_kernel(sample_batch, *refs):
    step_ref, gathered, refs = refs[0], refs[1:9], refs[9:]
    sources, refs = refs[:8], refs[8:]
    adjoint_out, packed_out, base_out, att_out, norms_out, bits_out, mods_out = refs[:7]
    weights, sems, in_sems, extra_sems, out_sems = refs[7:12]
    targets, refs = refs[12:20], refs[20:]
    hidden_ref, blocks, qgain_ref, kgain_ref, adjoint_ref, fgain_ref, wout_ref, win_ref = targets
    (
        mods,
        extra,
        up_wide,
        up_ref,
        down_wide,
        down_ref,
        base_u,
        att,
        norms,
        bits,
        blended,
        adj_u,
        adj_grad,
        low_grad,
    ) = refs
    tokens = adjoint_ref.shape[1]
    inner = 2 * weights.shape[4]
    half = inner // 2
    tiles = inner // LANES
    shards = weights.shape[2]
    turns = [slice(j * tokens, (j + 1) * tokens) for j in range(2)]
    gains = (qgain_ref, kgain_ref)
    core, _, _ = placement()
    early = load(sources[:4], targets[:4], in_sems)
    start_weights(gathered, weights, sems, range(4))
    extra_rows = pl.ds(gathered[0].shape[1] - extra.shape[2], extra.shape[2])
    late = load(
        [gathered[n].at[:, extra_rows, :] for n in (0, 4)],
        [extra.at[core], extra.at[1 - core]],
        extra_sems,
    )
    late += load(sources[4:], targets[4:], in_sems.at[pl.ds(4, 4)])

    def arrived(piece):
        wait_weights(gathered, weights, sems, piece)

    for copy in early:
        copy.wait()
    per = mods.shape[1] // 3 // half
    for o in range(3 * per):
        offset = 1.0 if o // per == 1 else 0.0
        mods[0:2, o * half : (o + 1) * half] = blocks[o] + offset
    normed = []
    for j, rs in enumerate(turns):
        hid = hidden_ref[rs, :]
        scaled = hid * row_norm(hid) * modulation(mods, j, 1) + modulation(mods, j, 0)
        normed.append(scaled.astype(BF))
    normed = jnp.concatenate(normed, axis=0)
    averager = head_averager()
    for part in range(2):
        arrived(part)
        raw = dot_nn(normed, qkv_block(weights, part))
        for i in range(tiles):
            x = raw[:, i * LANES : (i + 1) * LANES]
            r = lax.rsqrt(head_mean(x * x, averager) + EPS)
            z = x * r
            n = (z * gains[part][...]).astype(BF)
            for j, rs in enumerate(turns):
                norms[j, part, i] = z[rs]
                norms[j, 2 + part, i] = r[rs]
                bits[j, part, i] = n[rs]
    arrived(2)
    raw = dot_nn(normed, qkv_block(weights, 2)).astype(BF)
    for i in range(tiles):
        for j, rs in enumerate(turns):
            bits[j, 2, i] = raw[rs, i * LANES : (i + 1) * LANES]

    for i in range(tiles):
        for j, rs in enumerate(turns):
            score = dot_nt(split_heads(bits[j, 0, i]), bits[j, 1, i]) * (1.0 / math.sqrt(HEAD_DIM))
            e = jnp.exp(score)
            a = e * (1.0 / jnp.sum(e, axis=-1, keepdims=True))
            att[j, i] = a
            ab = a.astype(BF)
            mixed = dot_nn(
                jnp.concatenate([ab[:tokens], ab[tokens:]], axis=1), split_heads(bits[j, 2, i])
            )
            blended[rs, i * LANES : (i + 1) * LANES] = mixed.astype(BF)

    for copy in late:
        copy.wait()
    for h in range(2):
        for f in range(0, shards, 2):
            pair = [extra[h, f + n].astype(F32) for n in range(2)]
            for b in range(2):
                cols = slice((2 * h + b) * half, (2 * h + b + 1) * half)
                up_wide[4 * f : 4 * f + 8, cols] = jnp.concatenate(
                    [block[4 * b : 4 * b + 4] for block in pair], axis=0
                )
            for n in range(2):
                for k in range(3):
                    row = 48 * (f + n) + 24 * h + 8 * k
                    down_wide[row : row + 8, :] = pair[n][8:16, k * LANES : (k + 1) * LANES]
    up_ref[...] = up_wide[...].astype(BF)
    down_ref[...] = down_wide[:, 0 : down_ref.shape[1]].astype(BF)

    fgain = fgain_ref[...]
    gates = [modulation(mods, j, 2) for j in range(2)]
    lowrank = dot_nn(blended[...], down_ref[...]).astype(BF)
    arrived(3)
    for h in range(2):
        cols = slice(h * inner, (h + 1) * inner)
        base = dot_nn(blended[...], proj_block(weights, h))
        extra = dot_nn(lowrank, up_ref[:, cols])
        for j, rs in enumerate(turns):
            gate = gates[j][:, cols]
            u = hidden_ref[rs, cols] + gate * base[rs]
            base_u[j, :, cols] = u
            adj_u[j, :, cols] = u + gate * extra[rs]

    outs = [
        pltpu.make_async_copy(source.at[1], target, out_sems.at[n])
        for n, (source, target) in enumerate(
            ((base_u, base_out), (att, att_out), (norms, norms_out), (bits, bits_out))
        )
    ]
    outs.append(pltpu.make_async_copy(mods, mods_out, out_sems.at[4]))
    for copy in outs:
        copy.start()

    def velocity(u):
        return dot_nt((u * row_norm(u) * fgain).astype(BF), wout_ref[...])

    def regression(j, current):
        time = turn_time(step_ref, j)
        sigma = jnp.sqrt(2.0 * (1.0 - time) / time)
        gap = velocity(adj_u[j]) - velocity(base_u[j])
        residual = 2.0 / sigma * gap + sigma * current
        cotangent = 4.0 * residual / (sigma * sample_batch)
        grad = (tail_back(adj_u[j], cotangent, wout_ref, fgain) * gates[j]).astype(BF)
        adj_grad[turns[j], :] = grad
        low_grad[turns[j], :] = dot_nt(grad, up_ref[...]).astype(BF)

    current = adjoint_ref[...].T
    regression(0, current)
    current = latent_step(
        current,
        1.0 / turn_time(step_ref, 0),
        gates[0],
        modulation(mods, 0, 1),
        hidden_ref.at[turns[0], :],
        lambda what: None,
        weights,
        base_u.at[0],
        att.at[0],
        norms.at[0],
        bits.at[0],
        gains,
        wout_ref,
        fgain,
        win_ref,
    )
    regression(1, current)
    adjoint_out[...] = current

    down_grad = dot_tn(blended[...], low_grad[...])
    up_grad = dot_tn(lowrank, adj_grad[...])
    blank = jnp.zeros((8, HEAD_DIM), F32)
    for h in range(2):
        for f in range(shards):
            up_rows = jnp.concatenate(
                [
                    up_grad[4 * f : 4 * f + 4, (2 * h + b) * half : (2 * h + b + 1) * half]
                    for b in range(2)
                ],
                axis=0,
            )
            row = 48 * f + 24 * h
            down_rows = [down_grad[row + 8 * k : row + 8 * k + 8] for k in range(3)] + [blank]
            down_rows = [jnp.concatenate(down_rows[n : n + 2], axis=1) for n in (0, 2)]
            packed_out[h, f] = jnp.concatenate([up_rows] + down_rows, axis=1).astype(BF)
    for copy in outs:
        copy.wait()


def second_kernel(*refs):
    step_ref, gathered, refs = refs[0], refs[1:9], refs[9:]
    sources, refs = refs[:12], refs[12:]
    adjoint_out, weights, sems, in_sems = refs[:4]
    targets = refs[4:]
    (
        base_u,
        adjoint_ref,
        mods,
        fgain_ref,
        wout_ref,
        att,
        norms,
        bits,
        qgain_ref,
        kgain_ref,
        hidden,
        win_ref,
    ) = targets
    tokens = adjoint_ref.shape[0]
    sources = list(sources)
    sources[10] = sources[10].at[pl.ds(tokens, tokens), :]
    loads = load(sources[:5], targets[:5], in_sems)
    start_weights(gathered, weights, sems, (3,))
    loads += load(sources[5:10], targets[5:10], in_sems.at[pl.ds(5, 5)])
    start_weights(gathered, weights, sems, range(3))
    loads += load(sources[10:], targets[10:], in_sems.at[pl.ds(10, 2)])
    for copy in loads[:5]:
        copy.wait()

    def wait(what):
        if what == "state":
            for copy in loads[5:10]:
                copy.wait()
        elif what == "hidden":
            for copy in loads[10:]:
                copy.wait()
        elif what != "base":
            wait_weights(gathered, weights, sems, what)

    result = latent_step(
        adjoint_ref[...],
        1.0 / turn_time(step_ref, 1),
        modulation(mods, 1, 2),
        modulation(mods, 1, 1),
        hidden,
        wait,
        weights,
        base_u,
        att,
        norms,
        bits,
        (qgain_ref, kgain_ref),
        wout_ref,
        fgain_ref[...],
        win_ref,
    )
    adjoint_out[...] = result.T


VMEM_LIMIT = 60 * 1024 * 1024


def state_shapes(tokens, width, inner):
    tiles = inner // LANES
    return (
        ((tokens, width), F32),
        ((tiles, 2 * tokens, tokens), F32),
        ((4, tiles, tokens, LANES), F32),
        ((3, tiles, tokens, LANES), BF),
    )


VMEM = pl.BlockSpec(memory_space=pltpu.VMEM)
SMEM = pl.BlockSpec(memory_space=pltpu.SMEM)
HBM = pl.BlockSpec(memory_space=pl.ANY)
DMA = pltpu.SemaphoreType.DMA


def like(arrays):
    return [pltpu.VMEM(a.shape, a.dtype) for a in arrays]


def step_pair_first(sample_batch, step, gathered, *rest):
    hidden, adjoint = rest[0], rest[4]
    chan, tokens = adjoint.shape
    rows, width = hidden.shape
    shards, _, half = gathered[0].shape
    per_qkv = width // shards
    inner, rank = 2 * half, HEAD_DIM
    state = state_shapes(tokens, width, inner)
    grads = (2, shards, 8, half + 2 * LANES)
    mods = (8, 3 * width)
    return pl.pallas_call(
        partial(first_kernel, sample_batch),
        out_shape=(jax.ShapeDtypeStruct((tokens, chan), F32), jax.ShapeDtypeStruct(grads, BF))
        + tuple(jax.ShapeDtypeStruct(*leaf) for leaf in state)
        + (jax.ShapeDtypeStruct(mods, F32),),
        in_specs=[SMEM] + [HBM] * (len(gathered) + len(rest)),
        out_specs=(VMEM, VMEM) + (HBM,) * (len(state) + 1),
        scratch_shapes=[
            pltpu.VMEM((2, 4, shards, per_qkv, half), BF),
            DMA((2, 4)),
            DMA((len(rest),)),
            DMA((2,)),
            DMA((len(state) + 1,)),
        ]
        + like(rest)
        + [
            pltpu.VMEM(mods, F32),
            pltpu.VMEM((2, shards, 16, half), BF),
            pltpu.VMEM((rank, width), F32),
            pltpu.VMEM((rank, width), BF),
            pltpu.VMEM((inner, LANES), F32),
            pltpu.VMEM((inner, rank), BF),
        ]
        + [pltpu.VMEM((2,) + shape, dtype) for shape, dtype in state]
        + [
            pltpu.VMEM((rows, inner), BF),
            pltpu.VMEM((2, tokens, width), F32),
            pltpu.VMEM((rows, width), BF),
            pltpu.VMEM((rows, rank), BF),
        ],
        compiler_params=pltpu.CompilerParams(vmem_limit_bytes=VMEM_LIMIT),
        cost_estimate=pl.CostEstimate(
            flops=5_000_000_000, bytes_accessed=20_000_000, transcendentals=400_000
        ),
    )(step, *gathered, *rest)


def step_pair_second(step, gathered, *rest):
    adjoint, hidden = rest[1], rest[10]
    tokens, chan = adjoint.shape
    width = hidden.shape[1]
    shards, _, half = gathered[0].shape
    scratch = like(rest)
    scratch[10] = pltpu.VMEM((tokens, width), F32)
    return pl.pallas_call(
        second_kernel,
        out_shape=jax.ShapeDtypeStruct((chan, tokens), F32),
        in_specs=[SMEM] + [HBM] * (len(gathered) + len(rest)),
        out_specs=VMEM,
        scratch_shapes=[
            pltpu.VMEM((2, 4, shards, width // shards, half), BF),
            DMA((2, 4)),
            DMA((len(rest),)),
        ]
        + scratch,
        compiler_params=pltpu.CompilerParams(vmem_limit_bytes=VMEM_LIMIT),
        cost_estimate=pl.CostEstimate(
            flops=3_000_000_000, bytes_accessed=20_000_000, transcendentals=0
        ),
    )(step, *gathered, *rest)


def pieces_kernel(step_ref, *refs):
    sources, out = refs[:5], refs[5]
    targets, extra, in_sems = refs[6:11], refs[11], refs[12]
    qkv_ref, proj_ref, time_ref, up_ref, down_ref = targets
    loads = load(sources, targets, in_sems)
    core, plane, _ = placement()
    shards, _, half = out.shape
    rows, per_proj, time_rows = qkv_ref.shape[0], proj_ref.shape[0], time_ref.shape[0]
    owners = time_ref.shape[1] // half
    first = rows + time_rows

    def columns(start):
        return pl.ds(pl.multiple_of(start, LANES), half)

    for copy in loads:
        copy.wait()
    for b in range(2):
        extra[4 * b : 4 * b + 4, :] = up_ref[:, columns((2 * core + b) * half)].astype(F32)
    extra[8:16, :] = jnp.full((8, half), step_ref[0], jnp.int32).astype(F32)
    down = down_ref[...].astype(F32)
    down = jnp.where(core == 0, down[:24], down[24:])
    for k in range(3):
        extra[8:16, k * LANES : k * LANES + down.shape[1]] = down[8 * k : 8 * k + 8]
    extra_bits = extra[...].astype(BF)

    for r in range(shards):
        piece = (plane + r // Y_CHIPS + 2 * (r % Y_CHIPS)) & 3

        @pl.when(piece < 3)
        def _():
            out[r, 0:rows, :] = qkv_ref[:, columns((2 * piece + core) * half)]

        @pl.when(piece == 3)
        def _():
            for b in range(2):
                out[r, b * per_proj : (b + 1) * per_proj, :] = proj_ref[
                    :, columns((2 * core + b) * half)
                ]

        owned = min(r, owners - 1)
        out[r, rows:first, :] = time_ref[:, owned * half : (owned + 1) * half]
        out[r, first : first + 16, :] = extra_bits


def pieces_for(step, qkv, proj, time, up, down, shards):
    half = proj.shape[1] // 4
    shape = (shards, qkv.shape[0] + time.shape[0] + 16, half)
    inputs = (qkv, proj, time, up, down)
    return pl.pallas_call(
        pieces_kernel,
        out_shape=jax.ShapeDtypeStruct(shape, BF),
        in_specs=[SMEM] + [HBM] * len(inputs),
        out_specs=VMEM,
        scratch_shapes=like(inputs)
        + [pltpu.VMEM((16, half), F32), DMA((len(inputs),))],
        compiler_params=pltpu.CompilerParams(vmem_limit_bytes=VMEM_LIMIT),
    )(step, *inputs)


def gather_neighbours(home, mods, rows, dp, shards):
    z_chips = dp // 4

    def index(x, y, z, c):
        return ((x // 2 * z_chips + z) * 2 + c) * shards + (x % 2) * Y_CHIPS + y

    def neighbours(dx, dy, dz):
        return [
            (
                index((x + s * dx) % 4, (y + s * dy) % Y_CHIPS, (z + s * dz) % z_chips, c),
                index(x, y, z, c),
            )
            for x in range(4)
            for y in range(Y_CHIPS)
            for z in range(z_chips)
            for c, s in ((0, 1), (1, -1))
        ]

    swap = [(i, i ^ 1) for i in range(dp)]
    piece = home[:, :rows]
    parts = [
        lax.ppermute(piece, ("dp", "fsdp"), neighbours(*step))
        for step in ((0, 0, 1), (0, 1, 0), (-1, 0, 0))
    ]
    home, *parts[:2], mods = lax.optimization_barrier((home, *parts[:2], mods))
    own = [home] + parts
    return own + [lax.ppermute(block, "dp", swap) for block in own], mods


def time_features(upper_time):
    halves = TIME_FEAT // 2
    frequency = jnp.exp(-math.log(10000.0) * jnp.arange(halves, dtype=F32) / halves)
    angles = 1000.0 * upper_time[..., None] * frequency
    return jnp.concatenate([jnp.cos(angles), jnp.sin(angles)], axis=-1).astype(BF)


def per_device(
    states,
    adjoint,
    grid_step_index,
    input_weight,
    timestep_weight,
    query_key_value_weight,
    projection_weight,
    down_factor,
    up_factor,
    query_norm_gain,
    key_norm_gain,
    final_norm_gain,
    output_weight,
):
    dp, shards = lax.axis_size("dp"), lax.axis_size("fsdp")
    sample_batch = dp * shards * states.shape[0]
    core = lax.axis_index("dp") % 2
    tokens, chan = states.shape[2:]
    half = projection_weight.shape[1] // 4
    rows, time_rows = query_key_value_weight.shape[0], timestep_weight.shape[0]

    out = pieces_for(
        grid_step_index,
        query_key_value_weight,
        projection_weight,
        timestep_weight,
        up_factor,
        down_factor,
        shards,
    )
    home = lax.all_to_all(out, "fsdp", 0, 0, tiled=True)
    hidden = jnp.dot(states[0].reshape(2 * tokens, chan), input_weight, preferred_element_type=F32)
    gains = [jnp.tile(gain, 2)[None] for gain in (query_norm_gain, key_norm_gain)]
    fgain, wout = final_norm_gain[None], output_weight.T
    home, hidden, gains, fgain = lax.optimization_barrier((home, hidden, gains, fgain))

    steps = home[:, rows + time_rows + 8, HEAD_DIM].astype(F32)
    turns = jnp.arange(2, dtype=F32)
    feats = time_features((steps[:, None] + 1.0 - turns) / STEPS)
    mods = jnp.dot(
        feats.reshape(2 * shards, TIME_FEAT),
        home[:, rows : rows + time_rows].reshape(TIME_FEAT, half),
        preferred_element_type=F32,
    ).reshape(shards, 2, half)
    mods = lax.all_to_all(mods, "fsdp", 0, 0, tiled=True)
    gathered, mods = gather_neighbours(home, mods, rows, dp, shards)

    adjoint_mid, out, base, att, norms, bits, mods = step_pair_first(
        sample_batch,
        grid_step_index,
        gathered,
        hidden,
        mods,
        *gains,
        adjoint[0].T,
        fgain,
        wout,
        input_weight,
    )

    swap = [(i, i ^ 1) for i in range(dp)]
    chips = dp // 2
    out = out.reshape((2 * shards,) + out.shape[2:])
    groups = [
        [(2 * i + c) * shards + f for c in range(2) for f in range(shards)] for i in range(chips)
    ]
    got = lax.all_to_all(out, ("dp", "fsdp"), 0, 0, axis_index_groups=groups, tiled=True)
    adjoint_out = step_pair_second(
        grid_step_index,
        gathered,
        base,
        adjoint_mid,
        mods,
        fgain,
        wout,
        att,
        norms,
        bits,
        *gains,
        hidden,
        input_weight,
    )
    got, adjoint_out = lax.optimization_barrier((got, adjoint_out))
    part = jnp.sum(got.astype(F32), axis=0).astype(BF)
    got = lax.all_to_all(
        jnp.broadcast_to(part[None], (chips,) + part.shape),
        "dp",
        0,
        0,
        axis_index_groups=[[2 * i + c for i in range(chips)] for c in range(2)],
        tiled=True,
    )
    mine = jnp.sum(got.astype(F32), axis=0)
    theirs = lax.ppermute(mine, "dp", swap)
    halves = [jnp.where(core == 0, mine, theirs), jnp.where(core == 0, theirs, mine)]
    down_grad = [
        block[:, half + k * HEAD_DIM : half + (k + 1) * HEAD_DIM]
        for block in halves
        for k in range(3)
    ]
    up_grad = [block[4 * b : 4 * b + 4, :half] for block in halves for b in range(2)]
    return (
        adjoint_out.T[None],
        jnp.concatenate(down_grad, axis=0),
        jnp.concatenate(up_grad, axis=1),
    )


def solution(mesh):
    in_specs = (
        P(("dp", "fsdp"), None, None, None),
        P(("dp", "fsdp"), None, None),
        P(("dp", "fsdp")),
        P(),
        P("fsdp", None),
        P("fsdp", None),
        P("fsdp", None),
        P("fsdp", None),
        P("fsdp", None),
        P(),
        P(),
        P(),
        P(),
    )
    out_specs = (P(("dp", "fsdp"), None, None), P("fsdp", None), P("fsdp", None))
    return jax.shard_map(
        per_device, mesh=mesh, in_specs=in_specs, out_specs=out_specs, check_vma=False
    )
```

```python
from functools import partial
import math

import jax
import jax.numpy as jnp
from jax import lax
from jax.experimental import pallas as pl
from jax.experimental.pallas import tpu as pltpu
from jax.sharding import PartitionSpec as P

HEAD_DIM = 64
TIME_FEAT = 256
STEPS = 28
LANES = 128
EPS = 1e-06
Y_CHIPS = 8
BF = jnp.bfloat16
F32 = jnp.float32


def dot_nn(a, b):
    return lax.dot_general(a, b, (((1,), (0,)), ((), ())), preferred_element_type=F32)


def dot_nt(a, b):
    return lax.dot_general(a, b, (((1,), (1,)), ((), ())), preferred_element_type=F32)


def dot_tn(a, b):
    return lax.dot_general(a, b, (((0,), (0,)), ((), ())), preferred_element_type=F32)


def row_norm(u):
    return lax.rsqrt(jnp.mean(u * u, axis=-1, keepdims=True) + EPS)


def lane_index():
    return lax.broadcasted_iota(jnp.int32, (1, LANES), 1)


def split_heads(tile):
    even = (lane_index() < HEAD_DIM).astype(F32)
    return jnp.concatenate([tile * even.astype(BF), tile * (1.0 - even).astype(BF)], axis=0)


def head_averager():
    row = lax.broadcasted_iota(jnp.int32, (2 * LANES, LANES), 0) & (LANES - 1)
    col = lax.broadcasted_iota(jnp.int32, (2 * LANES, LANES), 1)
    same = ((row >= HEAD_DIM) == (col >= HEAD_DIM)).astype(F32)
    return (same * (1.0 / HEAD_DIM)).astype(BF)


def head_mean(values, averager):
    high = values.astype(BF)
    low = (values - high.astype(F32)).astype(BF)
    return dot_nn(jnp.concatenate([high, low], axis=1), averager)


def placement():
    z_chips = lax.axis_size("dp") // 4
    d, f = lax.axis_index("dp"), lax.axis_index("fsdp")
    core = lax.rem(d, 2)
    plane = 2 * lax.div(d, 2 * z_chips) + lax.rem(lax.div(d, 2), z_chips)
    return core, plane, (plane + lax.div(f, Y_CHIPS) + 2 * lax.rem(f, Y_CHIPS)) & 3


def load(sources, targets, sems):
    copies = [
        pltpu.make_async_copy(source, target, sems.at[n])
        for n, (source, target) in enumerate(zip(sources, targets, strict=True))
    ]
    for copy in copies:
        copy.start()
    return copies


def modulation(mods, j, which):
    width = mods.shape[1] // 3
    return mods[j : j + 1, which * width : (which + 1) * width]


def turn_time(step_ref, j):
    return (jnp.full((1, 1), step_ref[0], jnp.int32) + (1 - j)).astype(F32) / STEPS


def start_weights(gathered, weights, sems, pieces):
    core, _, color = placement()
    rows = pl.ds(0, weights.shape[3])
    for piece in pieces:
        for side, blocks in ((core, gathered[:4]), (1 - core, gathered[4:])):
            for n, block in enumerate(blocks):
                held = color if n == 0 else (color + jnp.where(side == 0, n, 4 - n)) & 3

                @pl.when(held == piece)
                def _():
                    pltpu.make_async_copy(
                        block.at[:, rows, :], weights.at[side, piece], sems.at[side, piece]
                    ).start()


def wait_weights(gathered, weights, sems, piece):
    for h in range(2):
        pltpu.make_async_copy(
            gathered[0].at[:, pl.ds(0, weights.shape[3]), :],
            weights.at[h, piece],
            sems.at[h, piece],
        ).wait()


def qkv_block(weights, part):
    half = weights.shape[4]
    return jnp.concatenate([weights[h, part].reshape(-1, half) for h in range(2)], axis=1)


def proj_block(weights, h):
    half, rows = weights.shape[4], weights.shape[3] // 2
    return jnp.concatenate(
        [weights[h, 3, :, b * rows : (b + 1) * rows, :].reshape(-1, half) for b in range(2)],
        axis=1,
    )


def tail_back(u, cotangent, wout_ref, fgain):
    dz = dot_nn(cotangent.astype(BF), wout_ref[...]) * fgain
    r = row_norm(u)
    z = u * r
    return r * (dz - z * jnp.mean(dz * z, axis=-1, keepdims=True))


def latent_step(
    current, decay, gate, scale1, hidden, wait, weights, base_u, att, norms, bits, gains, wout_ref,
    fgain, win_ref,
):
    tokens = current.shape[0]
    inner = weights.shape[4] * 2
    tiles = inner // LANES
    averager = head_averager()
    wait("base")
    hidden_grad = tail_back(base_u[...], current, wout_ref, fgain)
    proj_grad = (hidden_grad * gate).astype(BF)
    wait(3)
    blend_grad = jnp.zeros((tokens, inner), F32)
    for h in range(2):
        blend_grad = blend_grad + dot_nt(
            proj_grad[:, h * inner : (h + 1) * inner], proj_block(weights, h)
        )
    blend_grad = blend_grad.astype(BF)

    wait("state")
    grads = [[], [], []]
    for i in range(tiles):
        db = split_heads(blend_grad[:, i * LANES : (i + 1) * LANES])
        a = att[i]
        da = dot_nt(db, bits[2, i])
        ds = a * (da - jnp.sum(da * a, axis=-1, keepdims=True))
        ds = (ds * (1.0 / math.sqrt(HEAD_DIM))).astype(BF)
        grads[2].append(dot_tn(a.astype(BF), db).astype(BF))
        dq = dot_nn(ds, bits[1, i])
        dq = jnp.where(lane_index() < HEAD_DIM, dq[:tokens], dq[tokens:])
        dk = dot_tn(ds, split_heads(bits[0, i]))
        for n, grad in enumerate((dq, dk)):
            dz = grad * gains[n][...]
            z = norms[n, i]
            mean = head_mean(dz * z, averager)
            grads[n].append((norms[2 + n, i] * (dz - z * mean)).astype(BF))
    normed_grad = None
    for part in range(3):
        wait(part)
        term = dot_nt(jnp.concatenate(grads[part], axis=1), qkv_block(weights, part))
        normed_grad = term if normed_grad is None else normed_grad + term

    wait("hidden")
    hid = hidden[...]
    rh = row_norm(hid)
    hn = hid * rh
    dhn = normed_grad * scale1
    total = hidden_grad + rh * (dhn - hn * jnp.mean(dhn * hn, axis=-1, keepdims=True))
    latent_grad = dot_nt(total.astype(BF), win_ref[...])
    return current + (2.0 * latent_grad - current * decay) * (1.0 / STEPS)


def first_kernel(sample_batch, *refs):
    step_ref, gathered, refs = refs[0], refs[1:9], refs[9:]
    sources, refs = refs[:8], refs[8:]
    adjoint_out, packed_out, base_out, att_out, norms_out, bits_out, mods_out = refs[:7]
    weights, sems, in_sems, extra_sems, out_sems = refs[7:12]
    targets, refs = refs[12:20], refs[20:]
    hidden_ref, blocks, qgain_ref, kgain_ref, adjoint_ref, fgain_ref, wout_ref, win_ref = targets
    (
        mods,
        extra,
        up_wide,
        up_ref,
        down_wide,
        down_ref,
        base_u,
        att,
        norms,
        bits,
        blended,
        adj_u,
        adj_grad,
        low_grad,
    ) = refs
    tokens = adjoint_ref.shape[1]
    inner = 2 * weights.shape[4]
    half = inner // 2
    tiles = inner // LANES
    shards = weights.shape[2]
    turns = [slice(j * tokens, (j + 1) * tokens) for j in range(2)]
    gains = (qgain_ref, kgain_ref)
    core, _, _ = placement()
    early = load(sources[:4], targets[:4], in_sems)
    start_weights(gathered, weights, sems, range(4))
    extra_rows = pl.ds(gathered[0].shape[1] - extra.shape[2], extra.shape[2])
    late = load(
        [gathered[n].at[:, extra_rows, :] for n in (0, 4)],
        [extra.at[core], extra.at[1 - core]],
        extra_sems,
    )
    late += load(sources[4:], targets[4:], in_sems.at[pl.ds(4, 4)])

    def arrived(piece):
        wait_weights(gathered, weights, sems, piece)

    for copy in early:
        copy.wait()
    per = mods.shape[1] // 3 // half
    for o in range(3 * per):
        offset = 1.0 if o // per == 1 else 0.0
        mods[0:2, o * half : (o + 1) * half] = blocks[o] + offset
    normed = []
    for j, rs in enumerate(turns):
        hid = hidden_ref[rs, :]
        scaled = hid * row_norm(hid) * modulation(mods, j, 1) + modulation(mods, j, 0)
        normed.append(scaled.astype(BF))
    normed = jnp.concatenate(normed, axis=0)
    averager = head_averager()
    for part in range(2):
        arrived(part)
        raw = dot_nn(normed, qkv_block(weights, part))
        for i in range(tiles):
            x = raw[:, i * LANES : (i + 1) * LANES]
            r = lax.rsqrt(head_mean(x * x, averager) + EPS)
            z = x * r
            n = (z * gains[part][...]).astype(BF)
            for j, rs in enumerate(turns):
                norms[j, part, i] = z[rs]
                norms[j, 2 + part, i] = r[rs]
                bits[j, part, i] = n[rs]
    arrived(2)
    raw = dot_nn(normed, qkv_block(weights, 2)).astype(BF)
    for i in range(tiles):
        for j, rs in enumerate(turns):
            bits[j, 2, i] = raw[rs, i * LANES : (i + 1) * LANES]

    for i in range(tiles):
        for j, rs in enumerate(turns):
            score = dot_nt(split_heads(bits[j, 0, i]), bits[j, 1, i]) * (1.0 / math.sqrt(HEAD_DIM))
            e = jnp.exp(score)
            a = e * (1.0 / jnp.sum(e, axis=-1, keepdims=True))
            att[j, i] = a
            ab = a.astype(BF)
            mixed = dot_nn(
                jnp.concatenate([ab[:tokens], ab[tokens:]], axis=1), split_heads(bits[j, 2, i])
            )
            blended[rs, i * LANES : (i + 1) * LANES] = mixed.astype(BF)

    for copy in late:
        copy.wait()
    for h in range(2):
        for f in range(0, shards, 2):
            pair = [extra[h, f + n].astype(F32) for n in range(2)]
            for b in range(2):
                cols = slice((2 * h + b) * half, (2 * h + b + 1) * half)
                up_wide[4 * f : 4 * f + 8, cols] = jnp.concatenate(
                    [block[4 * b : 4 * b + 4] for block in pair], axis=0
                )
            for n in range(2):
                for k in range(3):
                    row = 48 * (f + n) + 24 * h + 8 * k
                    down_wide[row : row + 8, :] = pair[n][8:16, k * LANES : (k + 1) * LANES]
    up_ref[...] = up_wide[...].astype(BF)
    down_ref[...] = down_wide[:, 0 : down_ref.shape[1]].astype(BF)

    fgain = fgain_ref[...]
    gates = [modulation(mods, j, 2) for j in range(2)]
    lowrank = dot_nn(blended[...], down_ref[...]).astype(BF)
    arrived(3)
    for h in range(2):
        cols = slice(h * inner, (h + 1) * inner)
        base = dot_nn(blended[...], proj_block(weights, h))
        extra = dot_nn(lowrank, up_ref[:, cols])
        for j, rs in enumerate(turns):
            gate = gates[j][:, cols]
            u = hidden_ref[rs, cols] + gate * base[rs]
            base_u[j, :, cols] = u
            adj_u[j, :, cols] = u + gate * extra[rs]

    outs = [
        pltpu.make_async_copy(source.at[1], target, out_sems.at[n])
        for n, (source, target) in enumerate(
            ((base_u, base_out), (att, att_out), (norms, norms_out), (bits, bits_out))
        )
    ]
    outs.append(pltpu.make_async_copy(mods, mods_out, out_sems.at[4]))
    for copy in outs:
        copy.start()

    def velocity(u):
        return dot_nt((u * row_norm(u) * fgain).astype(BF), wout_ref[...])

    def regression(j, current):
        time = turn_time(step_ref, j)
        sigma = jnp.sqrt(2.0 * (1.0 - time) / time)
        gap = velocity(adj_u[j]) - velocity(base_u[j])
        residual = 2.0 / sigma * gap + sigma * current
        cotangent = 4.0 * residual / (sigma * sample_batch)
        grad = (tail_back(adj_u[j], cotangent, wout_ref, fgain) * gates[j]).astype(BF)
        adj_grad[turns[j], :] = grad
        low_grad[turns[j], :] = dot_nt(grad, up_ref[...]).astype(BF)

    current = adjoint_ref[...].T
    regression(0, current)
    current = latent_step(
        current,
        1.0 / turn_time(step_ref, 0),
        gates[0],
        modulation(mods, 0, 1),
        hidden_ref.at[turns[0], :],
        lambda what: None,
        weights,
        base_u.at[0],
        att.at[0],
        norms.at[0],
        bits.at[0],
        gains,
        wout_ref,
        fgain,
        win_ref,
    )
    regression(1, current)
    adjoint_out[...] = current

    down_grad = dot_tn(blended[...], low_grad[...])
    up_grad = dot_tn(lowrank, adj_grad[...])
    blank = jnp.zeros((8, HEAD_DIM), F32)
    for h in range(2):
        for f in range(shards):
            up_rows = jnp.concatenate(
                [
                    up_grad[4 * f : 4 * f + 4, (2 * h + b) * half : (2 * h + b + 1) * half]
                    for b in range(2)
                ],
                axis=0,
            )
            row = 48 * f + 24 * h
            down_rows = [down_grad[row + 8 * k : row + 8 * k + 8] for k in range(3)] + [blank]
            down_rows = [jnp.concatenate(down_rows[n : n + 2], axis=1) for n in (0, 2)]
            packed_out[h, f] = jnp.concatenate([up_rows] + down_rows, axis=1).astype(BF)
    for copy in outs:
        copy.wait()


def second_kernel(*refs):
    step_ref, gathered, refs = refs[0], refs[1:9], refs[9:]
    sources, refs = refs[:12], refs[12:]
    adjoint_out, weights, sems, in_sems = refs[:4]
    targets = refs[4:]
    (
        base_u,
        adjoint_ref,
        mods,
        fgain_ref,
        wout_ref,
        att,
        norms,
        bits,
        qgain_ref,
        kgain_ref,
        hidden,
        win_ref,
    ) = targets
    tokens = adjoint_ref.shape[0]
    sources = list(sources)
    sources[10] = sources[10].at[pl.ds(tokens, tokens), :]
    loads = load(sources[:5], targets[:5], in_sems)
    start_weights(gathered, weights, sems, (3,))
    loads += load(sources[5:10], targets[5:10], in_sems.at[pl.ds(5, 5)])
    start_weights(gathered, weights, sems, range(3))
    loads += load(sources[10:], targets[10:], in_sems.at[pl.ds(10, 2)])
    for copy in loads[:5]:
        copy.wait()

    def wait(what):
        if what == "state":
            for copy in loads[5:10]:
                copy.wait()
        elif what == "hidden":
            for copy in loads[10:]:
                copy.wait()
        elif what != "base":
            wait_weights(gathered, weights, sems, what)

    result = latent_step(
        adjoint_ref[...],
        1.0 / turn_time(step_ref, 1),
        modulation(mods, 1, 2),
        modulation(mods, 1, 1),
        hidden,
        wait,
        weights,
        base_u,
        att,
        norms,
        bits,
        (qgain_ref, kgain_ref),
        wout_ref,
        fgain_ref[...],
        win_ref,
    )
    adjoint_out[...] = result.T


VMEM_LIMIT = 60 * 1024 * 1024


def state_shapes(tokens, width, inner):
    tiles = inner // LANES
    return (
        ((tokens, width), F32),
        ((tiles, 2 * tokens, tokens), F32),
        ((4, tiles, tokens, LANES), F32),
        ((3, tiles, tokens, LANES), BF),
    )


VMEM = pl.BlockSpec(memory_space=pltpu.VMEM)
SMEM = pl.BlockSpec(memory_space=pltpu.SMEM)
HBM = pl.BlockSpec(memory_space=pl.ANY)
DMA = pltpu.SemaphoreType.DMA


def like(arrays):
    return [pltpu.VMEM(a.shape, a.dtype) for a in arrays]


def step_pair_first(sample_batch, step, gathered, *rest):
    hidden, adjoint = rest[0], rest[4]
    chan, tokens = adjoint.shape
    rows, width = hidden.shape
    shards, _, half = gathered[0].shape
    per_qkv = width // shards
    inner, rank = 2 * half, HEAD_DIM
    state = state_shapes(tokens, width, inner)
    grads = (2, shards, 8, half + 2 * LANES)
    mods = (8, 3 * width)
    return pl.pallas_call(
        partial(first_kernel, sample_batch),
        out_shape=(jax.ShapeDtypeStruct((tokens, chan), F32), jax.ShapeDtypeStruct(grads, BF))
        + tuple(jax.ShapeDtypeStruct(*leaf) for leaf in state)
        + (jax.ShapeDtypeStruct(mods, F32),),
        in_specs=[SMEM] + [HBM] * (len(gathered) + len(rest)),
        out_specs=(VMEM, VMEM) + (HBM,) * (len(state) + 1),
        scratch_shapes=[
            pltpu.VMEM((2, 4, shards, per_qkv, half), BF),
            DMA((2, 4)),
            DMA((len(rest),)),
            DMA((2,)),
            DMA((len(state) + 1,)),
        ]
        + like(rest)
        + [
            pltpu.VMEM(mods, F32),
            pltpu.VMEM((2, shards, 16, half), BF),
            pltpu.VMEM((rank, width), F32),
            pltpu.VMEM((rank, width), BF),
            pltpu.VMEM((inner, LANES), F32),
            pltpu.VMEM((inner, rank), BF),
        ]
        + [pltpu.VMEM((2,) + shape, dtype) for shape, dtype in state]
        + [
            pltpu.VMEM((rows, inner), BF),
            pltpu.VMEM((2, tokens, width), F32),
            pltpu.VMEM((rows, width), BF),
            pltpu.VMEM((rows, rank), BF),
        ],
        compiler_params=pltpu.CompilerParams(vmem_limit_bytes=VMEM_LIMIT),
        cost_estimate=pl.CostEstimate(
            flops=5_000_000_000, bytes_accessed=20_000_000, transcendentals=400_000
        ),
    )(step, *gathered, *rest)


def step_pair_second(step, gathered, *rest):
    adjoint, hidden = rest[1], rest[10]
    tokens, chan = adjoint.shape
    width = hidden.shape[1]
    shards, _, half = gathered[0].shape
    scratch = like(rest)
    scratch[10] = pltpu.VMEM((tokens, width), F32)
    return pl.pallas_call(
        second_kernel,
        out_shape=jax.ShapeDtypeStruct((chan, tokens), F32),
        in_specs=[SMEM] + [HBM] * (len(gathered) + len(rest)),
        out_specs=VMEM,
        scratch_shapes=[
            pltpu.VMEM((2, 4, shards, width // shards, half), BF),
            DMA((2, 4)),
            DMA((len(rest),)),
        ]
        + scratch,
        compiler_params=pltpu.CompilerParams(vmem_limit_bytes=VMEM_LIMIT),
        cost_estimate=pl.CostEstimate(
            flops=3_000_000_000, bytes_accessed=20_000_000, transcendentals=0
        ),
    )(step, *gathered, *rest)


def pieces_kernel(step_ref, *refs):
    sources, out = refs[:5], refs[5]
    targets, extra, in_sems = refs[6:11], refs[11], refs[12]
    qkv_ref, proj_ref, time_ref, up_ref, down_ref = targets
    loads = load(sources, targets, in_sems)
    core, plane, _ = placement()
    shards, _, half = out.shape
    rows, per_proj, time_rows = qkv_ref.shape[0], proj_ref.shape[0], time_ref.shape[0]
    owners = time_ref.shape[1] // half
    first = rows + time_rows

    def columns(start):
        return pl.ds(pl.multiple_of(start, LANES), half)

    for copy in loads:
        copy.wait()
    for b in range(2):
        extra[4 * b : 4 * b + 4, :] = up_ref[:, columns((2 * core + b) * half)].astype(F32)
    extra[8:16, :] = jnp.full((8, half), step_ref[0], jnp.int32).astype(F32)
    down = down_ref[...].astype(F32)
    down = jnp.where(core == 0, down[:24], down[24:])
    for k in range(3):
        extra[8:16, k * LANES : k * LANES + down.shape[1]] = down[8 * k : 8 * k + 8]
    extra_bits = extra[...].astype(BF)

    for r in range(shards):
        piece = (plane + r // Y_CHIPS + 2 * (r % Y_CHIPS)) & 3

        @pl.when(piece < 3)
        def _():
            out[r, 0:rows, :] = qkv_ref[:, columns((2 * piece + core) * half)]

        @pl.when(piece == 3)
        def _():
            for b in range(2):
                out[r, b * per_proj : (b + 1) * per_proj, :] = proj_ref[
                    :, columns((2 * core + b) * half)
                ]

        owned = min(r, owners - 1)
        out[r, rows:first, :] = time_ref[:, owned * half : (owned + 1) * half]
        out[r, first : first + 16, :] = extra_bits


def pieces_for(step, qkv, proj, time, up, down, shards):
    half = proj.shape[1] // 4
    shape = (shards, qkv.shape[0] + time.shape[0] + 16, half)
    inputs = (qkv, proj, time, up, down)
    return pl.pallas_call(
        pieces_kernel,
        out_shape=jax.ShapeDtypeStruct(shape, BF),
        in_specs=[SMEM] + [HBM] * len(inputs),
        out_specs=VMEM,
        scratch_shapes=like(inputs)
        + [pltpu.VMEM((16, half), F32), DMA((len(inputs),))],
        compiler_params=pltpu.CompilerParams(vmem_limit_bytes=VMEM_LIMIT),
    )(step, *inputs)


def gather_neighbours(home, mods, rows, dp, shards):
    z_chips = dp // 4

    def index(x, y, z, c):
        return ((x // 2 * z_chips + z) * 2 + c) * shards + (x % 2) * Y_CHIPS + y

    def neighbours(dx, dy, dz):
        return [
            (
                index((x + s * dx) % 4, (y + s * dy) % Y_CHIPS, (z + s * dz) % z_chips, c),
                index(x, y, z, c),
            )
            for x in range(4)
            for y in range(Y_CHIPS)
            for z in range(z_chips)
            for c, s in ((0, 1), (1, -1))
        ]

    swap = [(i, i ^ 1) for i in range(dp)]
    piece = home[:, :rows]
    parts = [
        lax.ppermute(piece, ("dp", "fsdp"), neighbours(*step))
        for step in ((1, 0, 0), (0, 1, 0), (0, 0, -1))
    ]
    home, *parts[:2], mods = lax.optimization_barrier((home, *parts[:2], mods))
    own = [home] + parts
    return own + [lax.ppermute(block, "dp", swap) for block in own], mods


def time_features(upper_time):
    halves = TIME_FEAT // 2
    frequency = jnp.exp(-math.log(10000.0) * jnp.arange(halves, dtype=F32) / halves)
    angles = 1000.0 * upper_time[..., None] * frequency
    return jnp.concatenate([jnp.cos(angles), jnp.sin(angles)], axis=-1).astype(BF)


def per_device(
    states,
    adjoint,
    grid_step_index,
    input_weight,
    timestep_weight,
    query_key_value_weight,
    projection_weight,
    down_factor,
    up_factor,
    query_norm_gain,
    key_norm_gain,
    final_norm_gain,
    output_weight,
):
    dp, shards = lax.axis_size("dp"), lax.axis_size("fsdp")
    sample_batch = dp * shards * states.shape[0]
    core = lax.axis_index("dp") % 2
    tokens, chan = states.shape[2:]
    half = projection_weight.shape[1] // 4
    rows, time_rows = query_key_value_weight.shape[0], timestep_weight.shape[0]

    out = pieces_for(
        grid_step_index,
        query_key_value_weight,
        projection_weight,
        timestep_weight,
        up_factor,
        down_factor,
        shards,
    )
    home = lax.all_to_all(out, "fsdp", 0, 0, tiled=True)
    hidden = jnp.dot(states[0].reshape(2 * tokens, chan), input_weight, preferred_element_type=F32)
    gains = [jnp.tile(gain, 2)[None] for gain in (query_norm_gain, key_norm_gain)]
    fgain, wout = final_norm_gain[None], output_weight.T
    home, hidden, gains, fgain = lax.optimization_barrier((home, hidden, gains, fgain))

    steps = home[:, rows + time_rows + 8, HEAD_DIM].astype(F32)
    turns = jnp.arange(2, dtype=F32)
    feats = time_features((steps[:, None] + 1.0 - turns) / STEPS)
    mods = jnp.dot(
        feats.reshape(2 * shards, TIME_FEAT),
        home[:, rows : rows + time_rows].reshape(TIME_FEAT, half),
        preferred_element_type=F32,
    ).reshape(shards, 2, half)
    mods = lax.all_to_all(mods, "fsdp", 0, 0, tiled=True)
    gathered, mods = gather_neighbours(home, mods, rows, dp, shards)

    adjoint_mid, out, base, att, norms, bits, mods = step_pair_first(
        sample_batch,
        grid_step_index,
        gathered,
        hidden,
        mods,
        *gains,
        adjoint[0].T,
        fgain,
        wout,
        input_weight,
    )

    swap = [(i, i ^ 1) for i in range(dp)]
    chips = dp // 2
    out = out.reshape((2 * shards,) + out.shape[2:])
    groups = [
        [(2 * i + c) * shards + f for c in range(2) for f in range(shards)] for i in range(chips)
    ]
    got = lax.all_to_all(out, ("dp", "fsdp"), 0, 0, axis_index_groups=groups, tiled=True)
    adjoint_out = step_pair_second(
        grid_step_index,
        gathered,
        base,
        adjoint_mid,
        mods,
        fgain,
        wout,
        att,
        norms,
        bits,
        *gains,
        hidden,
        input_weight,
    )
    got, adjoint_out = lax.optimization_barrier((got, adjoint_out))
    part = jnp.sum(got.astype(F32), axis=0).astype(BF)
    got = lax.all_to_all(
        jnp.broadcast_to(part[None], (chips,) + part.shape),
        "dp",
        0,
        0,
        axis_index_groups=[[2 * i + c for i in range(chips)] for c in range(2)],
        tiled=True,
    )
    mine = jnp.sum(got.astype(F32), axis=0)
    theirs = lax.ppermute(mine, "dp", swap)
    halves = [jnp.where(core == 0, mine, theirs), jnp.where(core == 0, theirs, mine)]
    down_grad = [
        block[:, half + k * HEAD_DIM : half + (k + 1) * HEAD_DIM]
        for block in halves
        for k in range(3)
    ]
    up_grad = [block[4 * b : 4 * b + 4, :half] for block in halves for b in range(2)]
    return (
        adjoint_out.T[None],
        jnp.concatenate(down_grad, axis=0),
        jnp.concatenate(up_grad, axis=1),
    )


def solution(mesh):
    in_specs = (
        P(("dp", "fsdp"), None, None, None),
        P(("dp", "fsdp"), None, None),
        P(("dp", "fsdp")),
        P(),
        P("fsdp", None),
        P("fsdp", None),
        P("fsdp", None),
        P("fsdp", None),
        P("fsdp", None),
        P(),
        P(),
        P(),
        P(),
    )
    out_specs = (P(("dp", "fsdp"), None, None), P("fsdp", None), P("fsdp", None))
    return jax.shard_map(
        per_device, mesh=mesh, in_specs=in_specs, out_specs=out_specs, check_vma=False
    )
```

```python
from functools import partial
import math

import jax
import jax.numpy as jnp
from jax import lax
from jax.experimental import pallas as pl
from jax.experimental.pallas import tpu as pltpu
from jax.sharding import PartitionSpec as P

HEAD_DIM = 64
TIME_FEAT = 256
STEPS = 28
LANES = 128
EPS = 1e-06
Y_CHIPS = 8
BF = jnp.bfloat16
F32 = jnp.float32


def dot_nn(a, b):
    return lax.dot_general(a, b, (((1,), (0,)), ((), ())), preferred_element_type=F32)


def dot_nt(a, b):
    return lax.dot_general(a, b, (((1,), (1,)), ((), ())), preferred_element_type=F32)


def dot_tn(a, b):
    return lax.dot_general(a, b, (((0,), (0,)), ((), ())), preferred_element_type=F32)


def row_norm(u):
    return lax.rsqrt(jnp.mean(u * u, axis=-1, keepdims=True) + EPS)


def lane_index():
    return lax.broadcasted_iota(jnp.int32, (1, LANES), 1)


def split_heads(tile):
    even = (lane_index() < HEAD_DIM).astype(F32)
    return jnp.concatenate([tile * even.astype(BF), tile * (1.0 - even).astype(BF)], axis=0)


def head_averager():
    row = lax.broadcasted_iota(jnp.int32, (2 * LANES, LANES), 0) & (LANES - 1)
    col = lax.broadcasted_iota(jnp.int32, (2 * LANES, LANES), 1)
    same = ((row >= HEAD_DIM) == (col >= HEAD_DIM)).astype(F32)
    return (same * (1.0 / HEAD_DIM)).astype(BF)


def head_mean(values, averager):
    high = values.astype(BF)
    low = (values - high.astype(F32)).astype(BF)
    return dot_nn(jnp.concatenate([high, low], axis=1), averager)


def placement():
    z_chips = lax.axis_size("dp") // 4
    d, f = lax.axis_index("dp"), lax.axis_index("fsdp")
    core = lax.rem(d, 2)
    plane = 2 * lax.div(d, 2 * z_chips) + lax.rem(lax.div(d, 2), z_chips)
    return core, plane, (plane + lax.div(f, Y_CHIPS) + 2 * lax.rem(f, Y_CHIPS)) & 3


def load(sources, targets, sems):
    copies = [
        pltpu.make_async_copy(source, target, sems.at[n])
        for n, (source, target) in enumerate(zip(sources, targets, strict=True))
    ]
    for copy in copies:
        copy.start()
    return copies


def modulation(mods, j, which):
    width = mods.shape[1] // 3
    return mods[j : j + 1, which * width : (which + 1) * width]


def turn_time(step_ref, j):
    return (jnp.full((1, 1), step_ref[0], jnp.int32) + (1 - j)).astype(F32) / STEPS


def start_weights(gathered, weights, sems, pieces):
    core, _, color = placement()
    rows = pl.ds(0, weights.shape[3])
    for piece in pieces:
        for side, blocks in ((core, gathered[:4]), (1 - core, gathered[4:])):
            for n, block in enumerate(blocks):
                held = color if n == 0 else (color + jnp.where(side == 0, n, 4 - n)) & 3

                @pl.when(held == piece)
                def _():
                    pltpu.make_async_copy(
                        block.at[:, rows, :], weights.at[side, piece], sems.at[side, piece]
                    ).start()


def wait_weights(gathered, weights, sems, piece):
    for h in range(2):
        pltpu.make_async_copy(
            gathered[0].at[:, pl.ds(0, weights.shape[3]), :],
            weights.at[h, piece],
            sems.at[h, piece],
        ).wait()


def qkv_block(weights, part):
    half = weights.shape[4]
    return jnp.concatenate([weights[h, part].reshape(-1, half) for h in range(2)], axis=1)


def proj_block(weights, h):
    half, rows = weights.shape[4], weights.shape[3] // 2
    return jnp.concatenate(
        [weights[h, 3, :, b * rows : (b + 1) * rows, :].reshape(-1, half) for b in range(2)],
        axis=1,
    )


def tail_back(u, cotangent, wout_ref, fgain):
    dz = dot_nn(cotangent.astype(BF), wout_ref[...]) * fgain
    r = row_norm(u)
    z = u * r
    return r * (dz - z * jnp.mean(dz * z, axis=-1, keepdims=True))


def latent_step(
    current, decay, gate, scale1, hidden, wait, weights, base_u, att, norms, bits, gains, wout_ref,
    fgain, win_ref,
):
    tokens = current.shape[0]
    inner = weights.shape[4] * 2
    tiles = inner // LANES
    averager = head_averager()
    wait("base")
    hidden_grad = tail_back(base_u[...], current, wout_ref, fgain)
    proj_grad = (hidden_grad * gate).astype(BF)
    wait(3)
    blend_grad = jnp.zeros((tokens, inner), F32)
    for h in range(2):
        blend_grad = blend_grad + dot_nt(
            proj_grad[:, h * inner : (h + 1) * inner], proj_block(weights, h)
        )
    blend_grad = blend_grad.astype(BF)

    wait("state")
    grads = [[], [], []]
    for i in range(tiles):
        db = split_heads(blend_grad[:, i * LANES : (i + 1) * LANES])
        a = att[i]
        da = dot_nt(db, bits[2, i])
        ds = a * (da - jnp.sum(da * a, axis=-1, keepdims=True))
        ds = (ds * (1.0 / math.sqrt(HEAD_DIM))).astype(BF)
        grads[2].append(dot_tn(a.astype(BF), db).astype(BF))
        dq = dot_nn(ds, bits[1, i])
        dq = jnp.where(lane_index() < HEAD_DIM, dq[:tokens], dq[tokens:])
        dk = dot_tn(ds, split_heads(bits[0, i]))
        for n, grad in enumerate((dq, dk)):
            dz = grad * gains[n][...]
            z = norms[n, i]
            mean = head_mean(dz * z, averager)
            grads[n].append((norms[2 + n, i] * (dz - z * mean)).astype(BF))
    normed_grad = None
    for part in range(3):
        wait(part)
        term = dot_nt(jnp.concatenate(grads[part], axis=1), qkv_block(weights, part))
        normed_grad = term if normed_grad is None else normed_grad + term

    wait("hidden")
    hid = hidden[...]
    rh = row_norm(hid)
    hn = hid * rh
    dhn = normed_grad * scale1
    total = hidden_grad + rh * (dhn - hn * jnp.mean(dhn * hn, axis=-1, keepdims=True))
    latent_grad = dot_nt(total.astype(BF), win_ref[...])
    return current + (2.0 * latent_grad - current * decay) * (1.0 / STEPS)


def first_kernel(sample_batch, *refs):
    step_ref, gathered, refs = refs[0], refs[1:9], refs[9:]
    sources, refs = refs[:8], refs[8:]
    adjoint_out, packed_out, base_out, att_out, norms_out, bits_out, mods_out = refs[:7]
    weights, sems, in_sems, extra_sems, out_sems = refs[7:12]
    targets, refs = refs[12:20], refs[20:]
    hidden_ref, blocks, qgain_ref, kgain_ref, adjoint_ref, fgain_ref, wout_ref, win_ref = targets
    (
        mods,
        extra,
        up_wide,
        up_ref,
        down_wide,
        down_ref,
        base_u,
        att,
        norms,
        bits,
        blended,
        adj_u,
        adj_grad,
        low_grad,
    ) = refs
    tokens = adjoint_ref.shape[1]
    inner = 2 * weights.shape[4]
    half = inner // 2
    tiles = inner // LANES
    shards = weights.shape[2]
    turns = [slice(j * tokens, (j + 1) * tokens) for j in range(2)]
    gains = (qgain_ref, kgain_ref)
    core, _, _ = placement()
    early = load(sources[:4], targets[:4], in_sems)
    start_weights(gathered, weights, sems, range(4))
    extra_rows = pl.ds(gathered[0].shape[1] - extra.shape[2], extra.shape[2])
    late = load(
        [gathered[n].at[:, extra_rows, :] for n in (0, 4)],
        [extra.at[core], extra.at[1 - core]],
        extra_sems,
    )
    late += load(sources[4:], targets[4:], in_sems.at[pl.ds(4, 4)])

    def arrived(piece):
        wait_weights(gathered, weights, sems, piece)

    for copy in early:
        copy.wait()
    per = mods.shape[1] // 3 // half
    for o in range(3 * per):
        offset = 1.0 if o // per == 1 else 0.0
        mods[0:2, o * half : (o + 1) * half] = blocks[o] + offset
    normed = []
    for j, rs in enumerate(turns):
        hid = hidden_ref[rs, :]
        scaled = hid * row_norm(hid) * modulation(mods, j, 1) + modulation(mods, j, 0)
        normed.append(scaled.astype(BF))
    normed = jnp.concatenate(normed, axis=0)
    averager = head_averager()
    for part in range(2):
        arrived(part)
        raw = dot_nn(normed, qkv_block(weights, part))
        for i in range(tiles):
            x = raw[:, i * LANES : (i + 1) * LANES]
            r = lax.rsqrt(head_mean(x * x, averager) + EPS)
            z = x * r
            n = (z * gains[part][...]).astype(BF)
            for j, rs in enumerate(turns):
                norms[j, part, i] = z[rs]
                norms[j, 2 + part, i] = r[rs]
                bits[j, part, i] = n[rs]
    arrived(2)
    raw = dot_nn(normed, qkv_block(weights, 2)).astype(BF)
    for i in range(tiles):
        for j, rs in enumerate(turns):
            bits[j, 2, i] = raw[rs, i * LANES : (i + 1) * LANES]

    for i in range(tiles):
        for j, rs in enumerate(turns):
            score = dot_nt(split_heads(bits[j, 0, i]), bits[j, 1, i]) * (1.0 / math.sqrt(HEAD_DIM))
            e = jnp.exp(score)
            a = e * (1.0 / jnp.sum(e, axis=-1, keepdims=True))
            att[j, i] = a
            ab = a.astype(BF)
            mixed = dot_nn(
                jnp.concatenate([ab[:tokens], ab[tokens:]], axis=1), split_heads(bits[j, 2, i])
            )
            blended[rs, i * LANES : (i + 1) * LANES] = mixed.astype(BF)

    for copy in late:
        copy.wait()
    for h in range(2):
        for f in range(0, shards, 2):
            pair = [extra[h, f + n].astype(F32) for n in range(2)]
            for b in range(2):
                cols = slice((2 * h + b) * half, (2 * h + b + 1) * half)
                up_wide[4 * f : 4 * f + 8, cols] = jnp.concatenate(
                    [block[4 * b : 4 * b + 4] for block in pair], axis=0
                )
            for n in range(2):
                for k in range(3):
                    row = 48 * (f + n) + 24 * h + 8 * k
                    down_wide[row : row + 8, :] = pair[n][8:16, k * LANES : (k + 1) * LANES]
    up_ref[...] = up_wide[...].astype(BF)
    down_ref[...] = down_wide[:, 0 : down_ref.shape[1]].astype(BF)

    fgain = fgain_ref[...]
    gates = [modulation(mods, j, 2) for j in range(2)]
    lowrank = dot_nn(blended[...], down_ref[...]).astype(BF)
    arrived(3)
    for h in range(2):
        cols = slice(h * inner, (h + 1) * inner)
        base = dot_nn(blended[...], proj_block(weights, h))
        extra = dot_nn(lowrank, up_ref[:, cols])
        for j, rs in enumerate(turns):
            gate = gates[j][:, cols]
            u = hidden_ref[rs, cols] + gate * base[rs]
            base_u[j, :, cols] = u
            adj_u[j, :, cols] = u + gate * extra[rs]

    outs = [
        pltpu.make_async_copy(source.at[1], target, out_sems.at[n])
        for n, (source, target) in enumerate(
            ((base_u, base_out), (att, att_out), (norms, norms_out), (bits, bits_out))
        )
    ]
    outs.append(pltpu.make_async_copy(mods, mods_out, out_sems.at[4]))
    for copy in outs:
        copy.start()

    normed = [
        (u * row_norm(u) * fgain).astype(BF)
        for j in range(2)
        for u in (adj_u[j], base_u[j])
    ]
    velocity = dot_nt(jnp.concatenate(normed, axis=0), wout_ref[...])
    gaps = [
        velocity[2 * j * tokens : (2 * j + 1) * tokens]
        - velocity[(2 * j + 1) * tokens : (2 * j + 2) * tokens]
        for j in range(2)
    ]

    def regression(j, current):
        time = turn_time(step_ref, j)
        sigma = jnp.sqrt(2.0 * (1.0 - time) / time)
        residual = 2.0 / sigma * gaps[j] + sigma * current
        cotangent = 4.0 * residual / (sigma * sample_batch)
        grad = (tail_back(adj_u[j], cotangent, wout_ref, fgain) * gates[j]).astype(BF)
        adj_grad[turns[j], :] = grad
        low_grad[turns[j], :] = dot_nt(grad, up_ref[...]).astype(BF)

    current = adjoint_ref[...].T
    regression(0, current)
    current = latent_step(
        current,
        1.0 / turn_time(step_ref, 0),
        gates[0],
        modulation(mods, 0, 1),
        hidden_ref.at[turns[0], :],
        lambda what: None,
        weights,
        base_u.at[0],
        att.at[0],
        norms.at[0],
        bits.at[0],
        gains,
        wout_ref,
        fgain,
        win_ref,
    )
    regression(1, current)
    adjoint_out[...] = current

    down_grad = dot_tn(blended[...], low_grad[...])
    up_grad = dot_tn(lowrank, adj_grad[...])
    blank = jnp.zeros((8, HEAD_DIM), F32)
    for h in range(2):
        for f in range(shards):
            up_rows = jnp.concatenate(
                [
                    up_grad[4 * f : 4 * f + 4, (2 * h + b) * half : (2 * h + b + 1) * half]
                    for b in range(2)
                ],
                axis=0,
            )
            row = 48 * f + 24 * h
            down_rows = [down_grad[row + 8 * k : row + 8 * k + 8] for k in range(3)] + [blank]
            down_rows = [jnp.concatenate(down_rows[n : n + 2], axis=1) for n in (0, 2)]
            packed_out[h, f] = jnp.concatenate([up_rows] + down_rows, axis=1).astype(BF)
    for copy in outs:
        copy.wait()


def second_kernel(*refs):
    step_ref, gathered, refs = refs[0], refs[1:9], refs[9:]
    sources, refs = refs[:12], refs[12:]
    adjoint_out, weights, sems, in_sems = refs[:4]
    targets = refs[4:]
    (
        base_u,
        adjoint_ref,
        mods,
        fgain_ref,
        wout_ref,
        att,
        norms,
        bits,
        qgain_ref,
        kgain_ref,
        hidden,
        win_ref,
    ) = targets
    tokens = adjoint_ref.shape[0]
    sources = list(sources)
    sources[10] = sources[10].at[pl.ds(tokens, tokens), :]
    loads = load(sources[:5], targets[:5], in_sems)
    start_weights(gathered, weights, sems, (3,))
    loads += load(sources[5:10], targets[5:10], in_sems.at[pl.ds(5, 5)])
    start_weights(gathered, weights, sems, range(3))
    loads += load(sources[10:], targets[10:], in_sems.at[pl.ds(10, 2)])
    for copy in loads[:5]:
        copy.wait()

    def wait(what):
        if what == "state":
            for copy in loads[5:10]:
                copy.wait()
        elif what == "hidden":
            for copy in loads[10:]:
                copy.wait()
        elif what != "base":
            wait_weights(gathered, weights, sems, what)

    result = latent_step(
        adjoint_ref[...],
        1.0 / turn_time(step_ref, 1),
        modulation(mods, 1, 2),
        modulation(mods, 1, 1),
        hidden,
        wait,
        weights,
        base_u,
        att,
        norms,
        bits,
        (qgain_ref, kgain_ref),
        wout_ref,
        fgain_ref[...],
        win_ref,
    )
    adjoint_out[...] = result.T


VMEM_LIMIT = 60 * 1024 * 1024


def state_shapes(tokens, width, inner):
    tiles = inner // LANES
    return (
        ((tokens, width), F32),
        ((tiles, 2 * tokens, tokens), F32),
        ((4, tiles, tokens, LANES), F32),
        ((3, tiles, tokens, LANES), BF),
    )


VMEM = pl.BlockSpec(memory_space=pltpu.VMEM)
SMEM = pl.BlockSpec(memory_space=pltpu.SMEM)
HBM = pl.BlockSpec(memory_space=pl.ANY)
DMA = pltpu.SemaphoreType.DMA


def like(arrays):
    return [pltpu.VMEM(a.shape, a.dtype) for a in arrays]


def step_pair_first(sample_batch, step, gathered, *rest):
    hidden, adjoint = rest[0], rest[4]
    chan, tokens = adjoint.shape
    rows, width = hidden.shape
    shards, _, half = gathered[0].shape
    per_qkv = width // shards
    inner, rank = 2 * half, HEAD_DIM
    state = state_shapes(tokens, width, inner)
    grads = (2, shards, 8, half + 2 * LANES)
    mods = (8, 3 * width)
    return pl.pallas_call(
        partial(first_kernel, sample_batch),
        out_shape=(jax.ShapeDtypeStruct((tokens, chan), F32), jax.ShapeDtypeStruct(grads, BF))
        + tuple(jax.ShapeDtypeStruct(*leaf) for leaf in state)
        + (jax.ShapeDtypeStruct(mods, F32),),
        in_specs=[SMEM] + [HBM] * (len(gathered) + len(rest)),
        out_specs=(VMEM, VMEM) + (HBM,) * (len(state) + 1),
        scratch_shapes=[
            pltpu.VMEM((2, 4, shards, per_qkv, half), BF),
            DMA((2, 4)),
            DMA((len(rest),)),
            DMA((2,)),
            DMA((len(state) + 1,)),
        ]
        + like(rest)
        + [
            pltpu.VMEM(mods, F32),
            pltpu.VMEM((2, shards, 16, half), BF),
            pltpu.VMEM((rank, width), F32),
            pltpu.VMEM((rank, width), BF),
            pltpu.VMEM((inner, LANES), F32),
            pltpu.VMEM((inner, rank), BF),
        ]
        + [pltpu.VMEM((2,) + shape, dtype) for shape, dtype in state]
        + [
            pltpu.VMEM((rows, inner), BF),
            pltpu.VMEM((2, tokens, width), F32),
            pltpu.VMEM((rows, width), BF),
            pltpu.VMEM((rows, rank), BF),
        ],
        compiler_params=pltpu.CompilerParams(vmem_limit_bytes=VMEM_LIMIT),
        cost_estimate=pl.CostEstimate(
            flops=5_000_000_000, bytes_accessed=20_000_000, transcendentals=400_000
        ),
    )(step, *gathered, *rest)


def step_pair_second(step, gathered, *rest):
    adjoint, hidden = rest[1], rest[10]
    tokens, chan = adjoint.shape
    width = hidden.shape[1]
    shards, _, half = gathered[0].shape
    scratch = like(rest)
    scratch[10] = pltpu.VMEM((tokens, width), F32)
    return pl.pallas_call(
        second_kernel,
        out_shape=jax.ShapeDtypeStruct((chan, tokens), F32),
        in_specs=[SMEM] + [HBM] * (len(gathered) + len(rest)),
        out_specs=VMEM,
        scratch_shapes=[
            pltpu.VMEM((2, 4, shards, width // shards, half), BF),
            DMA((2, 4)),
            DMA((len(rest),)),
        ]
        + scratch,
        compiler_params=pltpu.CompilerParams(vmem_limit_bytes=VMEM_LIMIT),
        cost_estimate=pl.CostEstimate(
            flops=3_000_000_000, bytes_accessed=20_000_000, transcendentals=0
        ),
    )(step, *gathered, *rest)


def pieces_kernel(step_ref, *refs):
    sources, out = refs[:5], refs[5]
    targets, extra, in_sems = refs[6:11], refs[11], refs[12]
    qkv_ref, proj_ref, time_ref, up_ref, down_ref = targets
    loads = load(sources, targets, in_sems)
    core, plane, _ = placement()
    shards, _, half = out.shape
    rows, per_proj, time_rows = qkv_ref.shape[0], proj_ref.shape[0], time_ref.shape[0]
    owners = time_ref.shape[1] // half
    first = rows + time_rows

    def columns(start):
        return pl.ds(pl.multiple_of(start, LANES), half)

    for copy in loads:
        copy.wait()
    for b in range(2):
        extra[4 * b : 4 * b + 4, :] = up_ref[:, columns((2 * core + b) * half)].astype(F32)
    extra[8:16, :] = jnp.full((8, half), step_ref[0], jnp.int32).astype(F32)
    down = down_ref[...].astype(F32)
    down = jnp.where(core == 0, down[:24], down[24:])
    for k in range(3):
        extra[8:16, k * LANES : k * LANES + down.shape[1]] = down[8 * k : 8 * k + 8]
    extra_bits = extra[...].astype(BF)

    for r in range(shards):
        piece = (plane + r // Y_CHIPS + 2 * (r % Y_CHIPS)) & 3

        @pl.when(piece < 3)
        def _():
            out[r, 0:rows, :] = qkv_ref[:, columns((2 * piece + core) * half)]

        @pl.when(piece == 3)
        def _():
            for b in range(2):
                out[r, b * per_proj : (b + 1) * per_proj, :] = proj_ref[
                    :, columns((2 * core + b) * half)
                ]

        owned = min(r, owners - 1)
        out[r, rows:first, :] = time_ref[:, owned * half : (owned + 1) * half]
        out[r, first : first + 16, :] = extra_bits


def pieces_for(step, qkv, proj, time, up, down, shards):
    half = proj.shape[1] // 4
    shape = (shards, qkv.shape[0] + time.shape[0] + 16, half)
    inputs = (qkv, proj, time, up, down)
    return pl.pallas_call(
        pieces_kernel,
        out_shape=jax.ShapeDtypeStruct(shape, BF),
        in_specs=[SMEM] + [HBM] * len(inputs),
        out_specs=VMEM,
        scratch_shapes=like(inputs)
        + [pltpu.VMEM((16, half), F32), DMA((len(inputs),))],
        compiler_params=pltpu.CompilerParams(vmem_limit_bytes=VMEM_LIMIT),
    )(step, *inputs)


def gather_neighbours(home, mods, rows, dp, shards):
    z_chips = dp // 4

    def index(x, y, z, c):
        return ((x // 2 * z_chips + z) * 2 + c) * shards + (x % 2) * Y_CHIPS + y

    def neighbours(dx, dy, dz):
        return [
            (
                index((x + s * dx) % 4, (y + s * dy) % Y_CHIPS, (z + s * dz) % z_chips, c),
                index(x, y, z, c),
            )
            for x in range(4)
            for y in range(Y_CHIPS)
            for z in range(z_chips)
            for c, s in ((0, 1), (1, -1))
        ]

    swap = [(i, i ^ 1) for i in range(dp)]
    piece = home[:, :rows]
    parts = [
        lax.ppermute(piece, ("dp", "fsdp"), neighbours(*step))
        for step in ((1, 0, 0), (0, 1, 0), (0, 0, -1))
    ]
    home, *parts[:2], mods = lax.optimization_barrier((home, *parts[:2], mods))
    own = [home] + parts
    return own + [lax.ppermute(block, "dp", swap) for block in own], mods


def time_features(upper_time):
    halves = TIME_FEAT // 2
    frequency = jnp.exp(-math.log(10000.0) * jnp.arange(halves, dtype=F32) / halves)
    angles = 1000.0 * upper_time[..., None] * frequency
    return jnp.concatenate([jnp.cos(angles), jnp.sin(angles)], axis=-1).astype(BF)


def per_device(
    states,
    adjoint,
    grid_step_index,
    input_weight,
    timestep_weight,
    query_key_value_weight,
    projection_weight,
    down_factor,
    up_factor,
    query_norm_gain,
    key_norm_gain,
    final_norm_gain,
    output_weight,
):
    dp, shards = lax.axis_size("dp"), lax.axis_size("fsdp")
    sample_batch = dp * shards * states.shape[0]
    core = lax.axis_index("dp") % 2
    tokens, chan = states.shape[2:]
    half = projection_weight.shape[1] // 4
    rows, time_rows = query_key_value_weight.shape[0], timestep_weight.shape[0]

    out = pieces_for(
        grid_step_index,
        query_key_value_weight,
        projection_weight,
        timestep_weight,
        up_factor,
        down_factor,
        shards,
    )
    home = lax.all_to_all(out, "fsdp", 0, 0, tiled=True)
    hidden = jnp.dot(states[0].reshape(2 * tokens, chan), input_weight, preferred_element_type=F32)
    gains = [jnp.tile(gain, 2)[None] for gain in (query_norm_gain, key_norm_gain)]
    fgain, wout = final_norm_gain[None], output_weight.T
    home, hidden, gains, fgain = lax.optimization_barrier((home, hidden, gains, fgain))

    steps = home[:, rows + time_rows + 8, HEAD_DIM].astype(F32)
    turns = jnp.arange(2, dtype=F32)
    feats = time_features((steps[:, None] + 1.0 - turns) / STEPS)
    mods = jnp.dot(
        feats.reshape(2 * shards, TIME_FEAT),
        home[:, rows : rows + time_rows].reshape(TIME_FEAT, half),
        preferred_element_type=F32,
    ).reshape(shards, 2, half)
    mods = lax.all_to_all(mods, "fsdp", 0, 0, tiled=True)
    gathered, mods = gather_neighbours(home, mods, rows, dp, shards)

    adjoint_mid, out, base, att, norms, bits, mods = step_pair_first(
        sample_batch,
        grid_step_index,
        gathered,
        hidden,
        mods,
        *gains,
        adjoint[0].T,
        fgain,
        wout,
        input_weight,
    )

    swap = [(i, i ^ 1) for i in range(dp)]
    chips = dp // 2
    out = out.reshape((2 * shards,) + out.shape[2:])
    groups = [
        [(2 * i + c) * shards + f for c in range(2) for f in range(shards)] for i in range(chips)
    ]
    got = lax.all_to_all(out, ("dp", "fsdp"), 0, 0, axis_index_groups=groups, tiled=True)
    adjoint_out = step_pair_second(
        grid_step_index,
        gathered,
        base,
        adjoint_mid,
        mods,
        fgain,
        wout,
        att,
        norms,
        bits,
        *gains,
        hidden,
        input_weight,
    )
    got, adjoint_out = lax.optimization_barrier((got, adjoint_out))
    part = jnp.sum(got.astype(F32), axis=0).astype(BF)
    got = lax.all_to_all(
        jnp.broadcast_to(part[None], (chips,) + part.shape),
        "dp",
        0,
        0,
        axis_index_groups=[[2 * i + c for i in range(chips)] for c in range(2)],
        tiled=True,
    )
    mine = jnp.sum(got.astype(F32), axis=0)
    theirs = lax.ppermute(mine, "dp", swap)
    halves = [jnp.where(core == 0, mine, theirs), jnp.where(core == 0, theirs, mine)]
    down_grad = [
        block[:, half + k * HEAD_DIM : half + (k + 1) * HEAD_DIM]
        for block in halves
        for k in range(3)
    ]
    up_grad = [block[4 * b : 4 * b + 4, :half] for block in halves for b in range(2)]
    return (
        adjoint_out.T[None],
        jnp.concatenate(down_grad, axis=0),
        jnp.concatenate(up_grad, axis=1),
    )


def solution(mesh):
    in_specs = (
        P(("dp", "fsdp"), None, None, None),
        P(("dp", "fsdp"), None, None),
        P(("dp", "fsdp")),
        P(),
        P("fsdp", None),
        P("fsdp", None),
        P("fsdp", None),
        P("fsdp", None),
        P("fsdp", None),
        P(),
        P(),
        P(),
        P(),
    )
    out_specs = (P(("dp", "fsdp"), None, None), P("fsdp", None), P("fsdp", None))
    return jax.shard_map(
        per_device, mesh=mesh, in_specs=in_specs, out_specs=out_specs, check_vma=False
    )
```
